32 devices in a mesh: row: 2 (over core), col: 16 (over z, y, x).
Axes of the slice: x: 2, y: 2, z: 4, core: 2. Of those that a mesh axis runs over, the one named last changes fastest.
Arguments:
- features: bfloat16 [8192, 128], P(('row', 'col')), may hold values from -6 to 6
- weight: bfloat16 [128, 256], replicated, may hold values from -0.5 to 0.5
- bias_vector: float32 [256], replicated, may hold values from -3 to 3
- cotangent: bfloat16 [8192, 256], P(('row', 'col')), may hold values from -6 to 6
- degrees: int32 [8192], P(('row', 'col')), may hold values from 1 to 255
- adjacency_tiles: bfloat16 [2, 16, 128, 128, 128], P('row', 'col'), may hold values from 0 to 1, as said below
- tile_positions: int32 [2, 16, 128], P('row', 'col'), may hold values from 0 to 127, as said below
- tile_counts: int32 [2, 16], P('row', 'col'), may hold values from 16 to 128, as said below
Outputs:
- activations: bfloat16 [8192, 256], P(('row', 'col'))
- grad_features: bfloat16 [8192, 128], P(('row', 'col'))
- grad_weight: float32 [128, 256], replicated
- grad_bias: float32 [256], replicated
The draws below stay inside these ranges and needn't reach their ends.
Inputs may be any that keep to these rules, and one draw needn't show every extreme that they name: `tile_positions`: the first tile_counts[r, c] positions of device (r, c) are distinct; each position q stands for row block q // 4 and column block q % 4 of that device. `tile_counts`: some device has all 128 slots live. `adjacency_tiles`: entries are 0 or 1.
All inputs are finite; a program needn't handle non-finite values.
Results may differ from the reference program's by a relative error of at most 0.015.
Values may be sent and summed in bfloat16 or wider, within the bound.
No kernel may reach another device: no remote copies, remote signals or barrier semaphores. Data moves between devices by JAX's collectives and lax.ppermute only.
A program may use at most 128 MiB of HBM per device.

```python
import jax
import jax.numpy as jnp
from jax import lax

F_IN = 128
HID = 256
BLOCK = 128
BPD = 2
TILES_DEV = 128
RBLK = 32
CBLK = 4
NODES = 8192
N_ROW = 2
N_COL = 16


def draw_adjacency_tiles(key, part):
    key = jax.random.fold_in(key, 31)
    values = jax.random.uniform(key, (N_ROW, N_COL, TILES_DEV, BLOCK, BLOCK), jnp.float32)
    return (values < 0.2).astype(jnp.float32).astype(jnp.bfloat16)


def draw_tile_positions(key, part):
    key = jax.random.fold_in(key, 32)
    keys = jax.random.split(key, N_ROW * N_COL)
    chosen = jax.vmap(lambda single: jax.random.permutation(single, RBLK * CBLK)[:TILES_DEV])(keys)
    return chosen.reshape(N_ROW, N_COL, TILES_DEV).astype(jnp.int32)


def draw_tile_counts(key, part):
    key = jax.random.fold_in(key, 33)
    first, second = jax.random.split(key)
    drawn = jax.random.randint(first, (N_ROW * N_COL,), 0, 64, dtype=jnp.int32)
    counts = TILES_DEV // 8 + (TILES_DEV - TILES_DEV // 8) * drawn * drawn // 4032
    fullest = jax.random.randint(second, (), 0, N_ROW * N_COL, dtype=jnp.int32)
    counts = counts.at[fullest].set(TILES_DEV)
    return counts.reshape(N_ROW, N_COL).astype(jnp.int32)


def plant(values, rng, smallest, largest):
    index_at = [jax.random.randint(jax.random.fold_in(rng, axis), (), 0, length) for axis, length in enumerate(values.shape)]
    main_axis = values.shape.index(max(values.shape))
    next_to = index_at[:main_axis] + [(index_at[main_axis] + 1) % values.shape[main_axis]] + index_at[main_axis + 1:]
    return values.at[tuple(index_at)].set(smallest).at[tuple(next_to)].set(largest)


def level_of(key, shape, pieces, least, top_value):
    def one(dim, shards_of):
        steps = jax.random.uniform(jax.random.fold_in(jax.random.fold_in(key, 6), dim), (shards_of,), jnp.float32, least / len(pieces), top_value / len(pieces))
        return jnp.repeat(jnp.exp(steps), shape[dim] // shards_of).reshape((-1,) + (1,) * (len(shape) - dim - 1))

    loudness = one(*pieces[0])
    for cut in pieces[1:]:
        loudness = loudness * one(*cut)
    return loudness


def noise(rng, extent, spread, limit, pieces=(), kind=jnp.bfloat16):
    level = level_of(rng, extent, pieces, -0.22, 0.18) if pieces else 1.0
    values = jax.random.normal(rng, extent, jnp.float32) * spread * level
    return jnp.minimum(jnp.maximum(values, -limit), limit).astype(kind)


def setup_inputs(seed: int = 0) -> dict:
    key_list = jax.random.split(jax.random.key(seed), 9)
    features = noise(key_list[0], (NODES, F_IN), 1.0, 6.0, ((0, 32),))
    weight = noise(key_list[1], (F_IN, HID), F_IN ** -0.5, 0.5)
    bias_vector = noise(key_list[2], (HID,), 0.5, 3.0, (), jnp.float32)
    cotangent = noise(key_list[3], (NODES, HID), 1.0, 6.0, ((0, 32),))
    degrees = plant(jax.random.randint(key_list[4], (NODES,), 1, 256), jax.random.fold_in(key_list[4], 1), 1, 255).astype(jnp.int32)
    adjacency_tiles = draw_adjacency_tiles(jax.random.fold_in(key_list[8], 71), 0)
    tile_positions = draw_tile_positions(jax.random.fold_in(key_list[8], 71), 0)
    tile_counts = draw_tile_counts(jax.random.fold_in(key_list[8], 71), 0)
    return dict(features=features, weight=weight, bias_vector=bias_vector, cotangent=cotangent, degrees=degrees, adjacency_tiles=adjacency_tiles, tile_positions=tile_positions, tile_counts=tile_counts)


def aggregate(source, adjacency_tiles, tile_positions, tile_counts, transposed):
    columns = source.shape[1]
    blocks_all = NODES // BLOCK
    blocked = source.astype(jnp.float32).reshape(blocks_all, BLOCK, columns)
    devices = N_ROW * N_COL
    flat_tiles = adjacency_tiles.reshape(devices, TILES_DEV, BLOCK, BLOCK)
    flat_positions = tile_positions.reshape(devices, TILES_DEV)
    flat_counts = tile_counts.reshape(devices)
    slot_index = jnp.arange(TILES_DEV, dtype=jnp.int32)

    def advance(totals, scan_items):
        tile_data, positions, total_live, device = scan_items
        row_index = device // N_COL
        col_index = device % N_COL
        row_block = positions // CBLK
        col_block = positions % CBLK
        global_rows = (row_index * RBLK + row_block).astype(jnp.int32)
        global_cols = ((col_block // BPD * N_COL + col_index) * BPD + col_block % BPD).astype(jnp.int32)
        active = (slot_index < total_live).astype(jnp.float32)
        tile_values = tile_data.astype(jnp.float32)
        if transposed:
            picked = blocked[global_rows]
            contrib = jnp.einsum('tji,tjf->tif', tile_values, picked, precision=lax.Precision.HIGHEST)
            targets = global_cols
        else:
            picked = blocked[global_cols]
            contrib = jnp.einsum('tij,tjf->tif', tile_values, picked, precision=lax.Precision.HIGHEST)
            targets = global_rows
        contrib = contrib * active[:, None, None]
        return (totals.at[targets].add(contrib), None)
    start = jnp.zeros((blocks_all, BLOCK, columns), jnp.float32)
    totals, _ = lax.scan(advance, start, (flat_tiles, flat_positions, flat_counts, jnp.arange(devices, dtype=jnp.int32)))
    return totals.reshape(NODES, columns)

def reference(features, weight, bias_vector, cotangent, degrees, adjacency_tiles, tile_positions, tile_counts):
    scale_rows = lax.rsqrt(degrees.astype(jnp.float32))[:, None]
    scaled = (scale_rows * features.astype(jnp.float32)).astype(jnp.bfloat16)
    aggregated = aggregate(scaled, adjacency_tiles, tile_positions, tile_counts, False)
    hidden = scale_rows * aggregated
    weight_full = weight.astype(jnp.float32)
    preact = jnp.dot(hidden, weight_full, precision=lax.Precision.HIGHEST) + bias_vector[None, :]
    logistic = jax.nn.sigmoid(preact)
    activations = (preact * logistic).astype(jnp.bfloat16)
    grad_pre = cotangent.astype(jnp.float32) * logistic * (1.0 + preact * (1.0 - logistic))
    grad_bias = lax.optimization_barrier(jnp.sum(grad_pre, axis=0))
    grad_weight = jnp.dot(hidden.T, grad_pre, precision=lax.Precision.HIGHEST)
    grad_agg = scale_rows * jnp.dot(grad_pre, weight_full.T, precision=lax.Precision.HIGHEST)
    grad_scaled = aggregate(grad_agg, adjacency_tiles, tile_positions, tile_counts, True)
    grad_features = (scale_rows * grad_scaled).astype(jnp.bfloat16)
    return (activations, grad_features, grad_weight, grad_bias)
```

```python
import functools

import jax
import jax.numpy as jnp
from jax import lax
from jax.experimental import pallas as pl
from jax.experimental.pallas import tpu as pltpu
from jax.sharding import PartitionSpec as P

BLOCK = 128
VMEM_BYTES = 48 * 1024 * 1024
F32 = jnp.float32
BF16 = jnp.bfloat16


def other(index, step, size):
    if size & (size - 1) == 0:
        return index ^ step
    return (index + step) % size


def source(index, step, size):
    if size & (size - 1) == 0:
        return index ^ step
    return (index - step) % size


def params():
    return pltpu.CompilerParams(vmem_limit_bytes=VMEM_BYTES)


def in_hbm(values):
    return pltpu.with_memory_space_constraint(values, pltpu.HBM)


def dot(left, right, contract=((1,), (0,))):
    return lax.dot_general(left, right, (contract, ((), ())), preferred_element_type=F32)


def split_two(values):
    upper = values.astype(BF16)
    return upper, (values - upper.astype(F32)).astype(BF16)


def scale_columns(degrees_row, columns):
    row = lax.rsqrt(degrees_row.astype(F32))
    return row, jnp.transpose(jnp.broadcast_to(row, (columns, row.shape[1])))


def scale_kernel(degrees_hbm, features_hbm, out_ref, degrees_ref, features_ref, sems):
    copies = [
        pltpu.make_async_copy(degrees_hbm, degrees_ref, sems.at[0]),
        pltpu.make_async_copy(features_hbm, features_ref, sems.at[1]),
    ]
    for copy in copies:
        copy.start()
    for copy in copies:
        copy.wait()
    _, scale = scale_columns(degrees_ref[...], features_ref.shape[1])
    out_ref[...] = (scale * features_ref[...].astype(F32)).astype(BF16)


def scale_features(degrees_row, features):
    return pl.pallas_call(
        scale_kernel,
        out_shape=jax.ShapeDtypeStruct(features.shape, BF16),
        in_specs=[pl.BlockSpec(memory_space=pltpu.HBM)] * 2,
        scratch_shapes=[
            pltpu.VMEM(degrees_row.shape, degrees_row.dtype),
            pltpu.VMEM(features.shape, features.dtype),
            pltpu.SemaphoreType.DMA((2,)),
        ],
        compiler_params=params(),
        name="scale_features",
    )(in_hbm(degrees_row), in_hbm(features))


def densify_kernel(
    col_slots, positions_hbm, counts_ref, tiles_ref, out_ref, positions_ref, taken_ref, zero_ref, sems
):
    places = taken_ref.shape[0]
    live = counts_ref[0, 0]
    fetch = pltpu.make_async_copy(positions_hbm, positions_ref, sems.at[0])
    fetch.start()
    zero_ref[...] = jnp.zeros_like(zero_ref)

    def clear(place, carry):
        taken_ref[place] = 0
        return carry

    lax.fori_loop(0, places, clear, 0, unroll=8)
    fetch.wait()

    def target(place):
        if col_slots & (col_slots - 1) == 0:
            row = lax.shift_right_logical(place, col_slots.bit_length() - 1)
            column = place & (col_slots - 1)
        else:
            row, column = lax.div(place, col_slots), lax.rem(place, col_slots)
        return out_ref.at[row, :, pl.ds(pl.multiple_of(column * BLOCK, BLOCK), BLOCK)]

    def send(slot):
        place = positions_ref[0, 0, slot]
        taken_ref[place] = 1
        pltpu.make_async_copy(tiles_ref.at[slot], target(place), sems.at[1]).start()

    def send_many(group, carry):
        for step in range(8):
            send(group * 8 + step)
        return carry

    def send_one(slot, carry):
        send(slot)
        return carry

    groups = lax.shift_right_logical(live, 3)
    lax.fori_loop(0, groups, send_many, 0)
    lax.fori_loop(groups * 8, live, send_one, 0)

    def blank(place, carry):
        @pl.when(taken_ref[place] == 0)
        def _():
            pltpu.make_async_copy(zero_ref, target(place), sems.at[1]).start()

        return carry

    @pl.when(live < places)
    def _():
        lax.fori_loop(0, places, blank, 0, unroll=8)

    pltpu.make_async_copy(out_ref, out_ref, sems.at[1]).wait()


def densify(positions, counts, tiles, row_slots, col_slots):
    return pl.pallas_call(
        functools.partial(densify_kernel, col_slots),
        out_shape=jax.ShapeDtypeStruct((row_slots, BLOCK, col_slots * BLOCK), BF16),
        in_specs=[
            pl.BlockSpec(memory_space=pltpu.HBM),
            pl.BlockSpec(memory_space=pltpu.SMEM),
            pl.BlockSpec(memory_space=pltpu.HBM),
        ],
        out_specs=pl.BlockSpec(memory_space=pl.ANY),
        scratch_shapes=[
            pltpu.SMEM(positions.shape, jnp.int32),
            pltpu.SMEM((row_slots * col_slots,), jnp.int32),
            pltpu.VMEM((BLOCK, BLOCK), BF16),
            pltpu.SemaphoreType.DMA((2,)),
        ],
        compiler_params=params(),
        name="densify",
    )(in_hbm(positions), counts, tiles)


def spot(low):
    col = lax.axis_index("col")
    if low & (low - 1) == 0:
        return lax.axis_index("row"), lax.shift_right_logical(col, low.bit_length() - 1), col & (low - 1)
    return lax.axis_index("row"), lax.div(col, low), lax.rem(col, low)


def piece_columns(index, nodes):
    return pl.ds(pl.multiple_of(index * nodes, nodes), nodes)


def forward_kernel(steps, pieces, dense_ref, *refs):
    scaled, outs = refs[:pieces], refs[pieces:]
    high, low, nodes, _ = dense_ref.shape
    row, line, plane = spot(low)
    for step, onward_ref, here_ref in zip(steps, outs[::2], outs[1::2]):
        column = other(plane, step, low)
        for hop in (*far_first(high), 0):
            chunk = other(line, hop, high)
            total = None
            for piece in range(pieces):
                columns = piece_columns(source(row, piece, pieces), nodes)
                term = dot(dense_ref[chunk, column, :, columns], scaled[piece][...])
                total = term if total is None else total + term
            if hop:
                onward_ref[hop - 1] = total.astype(onward_ref.dtype)
            else:
                here_ref[...] = total.astype(here_ref.dtype)


def forward(dense, scaled, steps):
    high, _, nodes, _ = dense.shape
    pieces = len(scaled)
    width = scaled[0].shape[1]
    products = pl.pallas_call(
        functools.partial(forward_kernel, steps, pieces),
        out_shape=[
            jax.ShapeDtypeStruct(shape, BF16 if step else F32)
            for step in steps
            for shape in ((high - 1, nodes, width), (nodes, width))
        ],
        in_specs=[pl.BlockSpec(memory_space=pltpu.VMEM)] * (1 + pieces),
        compiler_params=params(),
        name="forward_product",
    )(dense, *scaled)
    return dict(zip(steps, zip(products[::2], products[1::2])))


def combine_kernel(count, *refs):
    arrays, outs = refs[:count], refs[count:]
    for hop, out_ref in enumerate(outs):
        out_ref[...] = tree_sum([array[hop].astype(F32) for array in arrays]).astype(out_ref.dtype)


def combine(arrays):
    hops, nodes, columns = arrays[0].shape
    return pl.pallas_call(
        functools.partial(combine_kernel, len(arrays)),
        out_shape=[jax.ShapeDtypeStruct((nodes, columns), BF16)] * hops,
        in_specs=[pl.BlockSpec(memory_space=pltpu.VMEM)] * len(arrays),
        compiler_params=params(),
        name="combine",
    )(*arrays)


def layer_kernel(count, *refs):
    degrees_ref, weight_ref, bias_ref, cotangent_ref = refs[count : count + 4]
    outgoing_ref, hidden_ref, preact_ref, grad_pre_ref = refs[count + 4 :]
    total = tree_sum([ref[...].astype(F32) for ref in refs[:count]])
    row, scale = scale_columns(degrees_ref[...], total.shape[1])
    hidden = scale * total
    weight = weight_ref[...]
    upper, lower = split_two(hidden)
    preact = dot(upper, weight) + dot(lower, weight) + bias_ref[...]
    logistic = 1.0 / (1.0 + jnp.exp(-preact))
    grad_pre = cotangent_ref[...].astype(F32) * logistic * (1.0 + preact * (1.0 - logistic))
    upper, lower = split_two(grad_pre)
    across = ((1,), (1,))
    back = dot(weight, upper, across) + dot(weight, lower, across)
    outgoing_ref[...] = (row * back).astype(BF16)
    hidden_ref[...] = hidden
    preact_ref[...] = preact
    grad_pre_ref[...] = grad_pre


def layer(shares, degrees_row, weight, bias_row, cotangent):
    nodes = degrees_row.shape[1]
    depth, width = weight.shape
    return pl.pallas_call(
        functools.partial(layer_kernel, len(shares)),
        out_shape=[
            jax.ShapeDtypeStruct((depth, nodes), BF16),
            jax.ShapeDtypeStruct((nodes, depth), F32),
            jax.ShapeDtypeStruct((nodes, width), F32),
            jax.ShapeDtypeStruct((nodes, width), F32),
        ],
        compiler_params=params(),
        name="layer",
    )(*shares, degrees_row, weight, bias_row, cotangent)


def results_kernel(hidden_ref, preact_ref, grad_pre_ref, activations_ref, terms_ref):
    preact = preact_ref[...]
    activations_ref[...] = (preact / (1.0 + jnp.exp(-preact))).astype(BF16)
    grad_pre = grad_pre_ref[...]
    grads = split_two(grad_pre)
    upper, lower = split_two(jnp.transpose(hidden_ref[...]))
    weight_term = dot(upper, grads[0]) + dot(lower, grads[0]) + dot(upper, grads[1])
    depth = weight_term.shape[0]
    terms_ref[0:depth, :] = weight_term.astype(BF16)
    bias_term = jnp.sum(grad_pre, axis=0, keepdims=True)
    terms_ref[depth:, :] = jnp.broadcast_to(bias_term, (16, bias_term.shape[1])).astype(BF16)


def results(hidden, preact, grad_pre):
    return pl.pallas_call(
        results_kernel,
        out_shape=[
            jax.ShapeDtypeStruct(preact.shape, BF16),
            jax.ShapeDtypeStruct((hidden.shape[1] + 16, preact.shape[1]), BF16),
        ],
        compiler_params=params(),
        name="results",
    )(hidden, preact, grad_pre)


def tree_sum(values):
    while len(values) > 1:
        values = [left + right for left, right in zip(values[::2], values[1::2])] + (
            values[-1:] if len(values) % 2 else []
        )
    return values[0]


def sum_kernel(*refs):
    refs[-1][...] = tree_sum([ref[...].astype(F32) for ref in refs[:-1]]).astype(BF16)


def sum_terms(items):
    return pl.pallas_call(
        sum_kernel,
        out_shape=jax.ShapeDtypeStruct(items[0].shape, BF16),
        compiler_params=params(),
        name="sum_terms",
    )(*items)


def stack_kernel(low, *refs):
    items, out_ref = refs[:-1], refs[-1]
    _, line, _ = spot(low)
    for step, item in enumerate(items):
        out_ref[source(line, step, len(items))] = item[...]


def stack_line(low, items):
    return pl.pallas_call(
        functools.partial(stack_kernel, low),
        out_shape=jax.ShapeDtypeStruct((len(items),) + items[0].shape, BF16),
        in_specs=[pl.BlockSpec(memory_space=pltpu.VMEM)] * len(items),
        compiler_params=params(),
        name="stack_line",
    )(*items)


def backward_kernel(steps, pieces, has_totals, dense_ref, *refs):
    stacks, inputs, outs = refs[: len(steps)], refs[len(steps) : -pieces], refs[-pieces:]
    terms = inputs[pieces if has_totals else 0 :]
    high, low, nodes, _ = dense_ref.shape
    row, _, plane = spot(low)
    for piece in range(pieces):
        columns = piece_columns(other(row, piece, pieces), nodes)
        total = inputs[piece][...] if has_totals else None
        for step, stack_ref in zip(steps, stacks):
            origin = source(plane, step, low)
            for chunk in range(high):
                term = dot(stack_ref[chunk], dense_ref[chunk, origin, :, columns])
                total = term if total is None else total + term
        depth = total.shape[0]
        outs[piece][0:depth, :] = total.astype(outs[piece].dtype)
        if terms and piece:
            outs[piece][depth:, :] = tree_sum([ref[...].astype(F32) for ref in terms]).astype(BF16)


def backward(dense, stacks, totals, terms=()):
    nodes, slots = dense.shape[2:]
    pieces = slots // nodes
    depth = next(iter(stacks.values())).shape[1]
    inputs = list(stacks.values()) + list(totals) + list(terms)

    def shape_of(piece):
        if terms and piece:
            return jax.ShapeDtypeStruct((depth + terms[0].shape[0], nodes), BF16)
        return jax.ShapeDtypeStruct((depth, nodes), F32)

    return pl.pallas_call(
        functools.partial(backward_kernel, tuple(stacks), pieces, bool(totals)),
        out_shape=[shape_of(piece) for piece in range(pieces)],
        in_specs=[pl.BlockSpec(memory_space=pltpu.VMEM)] * (1 + len(inputs)),
        compiler_params=params(),
        name="backward_product",
    )(dense, *inputs)


def finish_kernel(pieces, degrees_ref, own_ref, sent_ref, *refs):
    shares, outs = refs[: pieces - 1], refs[pieces - 1 :]
    total = own_ref[...]
    depth = total.shape[0]
    for share in shares:
        total = total + share[0:depth, :].astype(F32)
    row = lax.rsqrt(degrees_ref[...].astype(F32))
    outs[0][...] = jnp.transpose(row * total).astype(BF16)
    terms = tree_sum([ref[depth:, :].astype(F32) for ref in (sent_ref, *shares)])
    outs[1][...] = terms[0:depth]
    outs[2][...] = terms[depth : depth + 1]


def finish(degrees_row, own, sent, shares):
    depth, nodes = own.shape
    width = sent.shape[1]
    return pl.pallas_call(
        functools.partial(finish_kernel, len(shares) + 1),
        out_shape=[
            jax.ShapeDtypeStruct((nodes, depth), BF16),
            jax.ShapeDtypeStruct((depth, width), F32),
            jax.ShapeDtypeStruct((1, width), F32),
        ],
        compiler_params=params(),
        name="finish",
    )(degrees_row, own, sent, *shares)


def far_first(size):
    return range(size - 1, 0, -1)


def per_device(
    features, weight, bias_vector, cotangent, degrees, adjacency_tiles, tile_positions, tile_counts
):
    rows = lax.axis_size("row")
    cols = lax.axis_size("col")
    nodes = features.shape[0]
    per_part = nodes // BLOCK
    row_slots = cols * per_part
    col_slots = rows * per_part
    low = 4 if cols % 4 == 0 else 1
    high = cols // low

    degrees_row = degrees[None, :]

    def over_row(values, step):
        pairs = [(index, other(index, step, rows)) for index in range(rows)]
        return lax.ppermute(values, "row", pairs)

    def over_plane(values, step):
        pairs = [
            (index, index // low * low + other(index % low, step, low)) for index in range(cols)
        ]
        return lax.ppermute(values, "col", pairs)

    def over_line(values, step):
        pairs = [
            (index, other(index // low, step, high) * low + index % low) for index in range(cols)
        ]
        return lax.ppermute(values, "col", pairs)

    own = scale_features(degrees_row, features)
    scaled = [own] + [over_row(own, step) for step in range(1, rows)]
    dense = densify(
        tile_positions, tile_counts, adjacency_tiles[0, 0], row_slots, col_slots
    ).reshape(high, low, nodes, col_slots * BLOCK)

    products = forward(dense, scaled, (low - 1,)) | forward(dense, scaled, tuple(range(low - 1))[::-1])
    onward = [products[0][0]] + [over_plane(products[step][0], step) for step in far_first(low)]
    here = [products[0][1]] + [over_plane(products[step][1], step) for step in far_first(low)]
    chunks = combine(onward)
    shares = [over_line(chunks[hop - 1], hop) for hop in far_first(high)]
    outgoing, *kept = layer(here + shares, degrees_row, weight, bias_vector[None, :], cotangent)

    line = {0: outgoing} | {step: over_line(outgoing, step) for step in far_first(high)}
    activations, terms = results(*kept)
    parts = {0: terms} | {step: over_plane(terms, step) for step in far_first(low)}
    line, parts = lax.optimization_barrier((line, parts))
    stacked = stack_line(low, [line[step] for step in range(high)])
    terms = sum_terms([parts[step] for step in range(low)])
    stacks = {0: stacked} | {step: over_plane(stacked, step) for step in far_first(low)}
    parts = {0: terms} | {step: over_line(terms, step) for step in far_first(high)}
    terms = [parts[step] for step in range(high)]
    steps, totals = list(stacks), []
    for group in (steps[: low // 2], steps[low // 2 :]):
        if group:
            arrived = {step: stacks[step] for step in group}
            totals = backward(dense, arrived, totals, terms if group[-1] == steps[-1] else ())
    returned = [over_row(totals[step], step) for step in range(1, rows)]
    grad_features, grad_weight, grad_bias = finish(degrees_row, totals[0], totals[1], returned)
    return activations, grad_features, grad_weight, grad_bias[0]


def solution(mesh):
    placed = (
        P(("row", "col"), None),
        P(),
        P(),
        P(("row", "col"), None),
        P(("row", "col")),
        P("row", "col", None, None, None),
        P("row", "col", None),
        P("row", "col"),
    )
    return jax.shard_map(
        per_device,
        mesh=mesh,
        in_specs=placed,
        out_specs=(P(("row", "col"), None), P(("row", "col"), None), P(), P()),
        check_vma=False,
    )
```

```python
import functools

import jax
import jax.numpy as jnp
from jax import lax
from jax.experimental import pallas as pl
from jax.experimental.pallas import tpu as pltpu
from jax.sharding import PartitionSpec as P

BLOCK = 128
VMEM_BYTES = 48 * 1024 * 1024
F32 = jnp.float32
BF16 = jnp.bfloat16


def other(index, step, size):
    if size & (size - 1) == 0:
        return index ^ step
    return (index + step) % size


def source(index, step, size):
    if size & (size - 1) == 0:
        return index ^ step
    return (index - step) % size


def params():
    return pltpu.CompilerParams(vmem_limit_bytes=VMEM_BYTES)


def in_hbm(values):
    return pltpu.with_memory_space_constraint(values, pltpu.HBM)


def dot(left, right, contract=((1,), (0,))):
    return lax.dot_general(left, right, (contract, ((), ())), preferred_element_type=F32)


def split_two(values):
    upper = values.astype(BF16)
    return upper, (values - upper.astype(F32)).astype(BF16)


def scale_columns(degrees_row, columns):
    row = lax.rsqrt(degrees_row.astype(F32))
    return row, jnp.transpose(jnp.broadcast_to(row, (columns, row.shape[1])))


def densify_kernel(
    col_slots, positions_hbm, counts_ref, tiles_ref, out_ref, positions_ref, taken_ref, zero_ref, sems
):
    places = taken_ref.shape[0]
    live = counts_ref[0, 0]
    fetch = pltpu.make_async_copy(positions_hbm, positions_ref, sems.at[0])
    fetch.start()
    zero_ref[...] = jnp.zeros_like(zero_ref)

    def clear(place, carry):
        taken_ref[place] = 0
        return carry

    lax.fori_loop(0, places, clear, 0, unroll=8)
    fetch.wait()

    def target(place):
        if col_slots & (col_slots - 1) == 0:
            row = lax.shift_right_logical(place, col_slots.bit_length() - 1)
            column = place & (col_slots - 1)
        else:
            row, column = lax.div(place, col_slots), lax.rem(place, col_slots)
        return out_ref.at[row, :, pl.ds(pl.multiple_of(column * BLOCK, BLOCK), BLOCK)]

    def send(slot):
        place = positions_ref[0, 0, slot]
        taken_ref[place] = 1
        pltpu.make_async_copy(tiles_ref.at[slot], target(place), sems.at[1]).start()

    def send_many(group, carry):
        for step in range(8):
            send(group * 8 + step)
        return carry

    def send_one(slot, carry):
        send(slot)
        return carry

    groups = lax.shift_right_logical(live, 3)
    lax.fori_loop(0, groups, send_many, 0)
    lax.fori_loop(groups * 8, live, send_one, 0)

    def blank(place, carry):
        @pl.when(taken_ref[place] == 0)
        def _():
            pltpu.make_async_copy(zero_ref, target(place), sems.at[1]).start()

        return carry

    @pl.when(live < places)
    def _():
        lax.fori_loop(0, places, blank, 0, unroll=8)

    pltpu.make_async_copy(out_ref, out_ref, sems.at[1]).wait()


def densify(positions, counts, tiles, row_slots, col_slots):
    return pl.pallas_call(
        functools.partial(densify_kernel, col_slots),
        out_shape=jax.ShapeDtypeStruct((row_slots, BLOCK, col_slots * BLOCK), BF16),
        in_specs=[
            pl.BlockSpec(memory_space=pltpu.HBM),
            pl.BlockSpec(memory_space=pltpu.SMEM),
            pl.BlockSpec(memory_space=pltpu.HBM),
        ],
        out_specs=pl.BlockSpec(memory_space=pl.ANY),
        scratch_shapes=[
            pltpu.SMEM(positions.shape, jnp.int32),
            pltpu.SMEM((row_slots * col_slots,), jnp.int32),
            pltpu.VMEM((BLOCK, BLOCK), BF16),
            pltpu.SemaphoreType.DMA((2,)),
        ],
        compiler_params=params(),
        name="densify",
    )(in_hbm(positions), counts, tiles)


def spot(low):
    col = lax.axis_index("col")
    if low & (low - 1) == 0:
        return lax.axis_index("row"), lax.shift_right_logical(col, low.bit_length() - 1), col & (low - 1)
    return lax.axis_index("row"), lax.div(col, low), lax.rem(col, low)


def piece_columns(index, nodes):
    return pl.ds(pl.multiple_of(index * nodes, nodes), nodes)


def forward_kernel(wanted, pieces, scaling, dense_ref, *refs):
    inputs = refs[: 2 * pieces if scaling else pieces]
    outs = refs[len(inputs) :]
    high, low, nodes, _ = dense_ref.shape
    row, line, plane = spot(low)
    if scaling:
        scaled = outs[len(wanted) :]
        for degrees_ref, features_ref, out_ref in zip(inputs[:pieces], inputs[pieces:], scaled):
            _, scale = scale_columns(degrees_ref[...], features_ref.shape[1])
            out_ref[...] = (scale * features_ref[...].astype(F32)).astype(BF16)
    else:
        scaled = inputs

    def product(step, hop):
        column, chunk = other(plane, step, low), other(line, hop, high)
        total = None
        for piece in range(pieces):
            columns = piece_columns(source(row, piece, pieces), nodes)
            term = dot(dense_ref[chunk, column, :, columns], scaled[piece][...])
            total = term if total is None else total + term
        return total

    for (step, onward), out_ref in zip(wanted, outs):
        if onward:
            for hop in far_first(high):
                out_ref[hop - 1] = product(step, hop).astype(out_ref.dtype)
        else:
            out_ref[...] = product(step, 0).astype(out_ref.dtype)


def forward(dense, inputs, wanted, scaling=False):
    high, _, nodes, _ = dense.shape
    pieces = len(inputs) // 2 if scaling else len(inputs)
    width = inputs[-1].shape[1]

    def shape_of(step, onward):
        shape = (high - 1, nodes, width) if onward else (nodes, width)
        return jax.ShapeDtypeStruct(shape, BF16 if step else F32)

    outs = pl.pallas_call(
        functools.partial(forward_kernel, wanted, pieces, scaling),
        out_shape=[shape_of(*item) for item in wanted]
        + [jax.ShapeDtypeStruct((nodes, width), BF16)] * (pieces if scaling else 0),
        in_specs=[pl.BlockSpec(memory_space=pltpu.VMEM)] * (1 + len(inputs)),
        compiler_params=params(),
        name="forward_product",
    )(dense, *inputs)
    return dict(zip(wanted, outs)), outs[len(wanted) :]


def combine_kernel(count, *refs):
    arrays, outs = refs[:count], refs[count:]
    for hop, out_ref in enumerate(outs):
        out_ref[...] = tree_sum([array[hop].astype(F32) for array in arrays]).astype(out_ref.dtype)


def combine(arrays):
    hops, nodes, columns = arrays[0].shape
    return pl.pallas_call(
        functools.partial(combine_kernel, len(arrays)),
        out_shape=[jax.ShapeDtypeStruct((nodes, columns), BF16)] * hops,
        in_specs=[pl.BlockSpec(memory_space=pltpu.VMEM)] * len(arrays),
        compiler_params=params(),
        name="combine",
    )(*arrays)


def layer_kernel(count, *refs):
    degrees_ref, weight_ref, bias_ref, cotangent_ref = refs[count : count + 4]
    outgoing_ref, hidden_ref, preact_ref, grad_pre_ref = refs[count + 4 :]
    total = tree_sum([ref[...].astype(F32) for ref in refs[:count]])
    row, scale = scale_columns(degrees_ref[...], total.shape[1])
    hidden = scale * total
    weight = weight_ref[...]
    upper, lower = split_two(hidden)
    preact = dot(upper, weight) + dot(lower, weight) + bias_ref[...]
    logistic = 1.0 / (1.0 + jnp.exp(-preact))
    grad_pre = cotangent_ref[...].astype(F32) * logistic * (1.0 + preact * (1.0 - logistic))
    upper, lower = split_two(grad_pre)
    across = ((1,), (1,))
    back = dot(weight, upper, across) + dot(weight, lower, across)
    outgoing_ref[...] = (row * back).astype(BF16)
    hidden_ref[...] = hidden
    preact_ref[...] = preact
    grad_pre_ref[...] = grad_pre


def layer(shares, degrees_row, weight, bias_row, cotangent):
    nodes = degrees_row.shape[1]
    depth, width = weight.shape
    return pl.pallas_call(
        functools.partial(layer_kernel, len(shares)),
        out_shape=[
            jax.ShapeDtypeStruct((depth, nodes), BF16),
            jax.ShapeDtypeStruct((nodes, depth), F32),
            jax.ShapeDtypeStruct((nodes, width), F32),
            jax.ShapeDtypeStruct((nodes, width), F32),
        ],
        compiler_params=params(),
        name="layer",
    )(*shares, degrees_row, weight, bias_row, cotangent)


def activations_kernel(preact_ref, out_ref):
    preact = preact_ref[...]
    out_ref[...] = (preact / (1.0 + jnp.exp(-preact))).astype(BF16)


def activations_of(preact):
    return pl.pallas_call(
        activations_kernel,
        out_shape=jax.ShapeDtypeStruct(preact.shape, BF16),
        compiler_params=params(),
        name="activations",
    )(preact)


def terms_kernel(hidden_ref, grad_pre_ref, terms_ref):
    grad_pre = grad_pre_ref[...]
    grads = split_two(grad_pre)
    upper, lower = split_two(jnp.transpose(hidden_ref[...]))
    weight_term = dot(upper, grads[0]) + dot(lower, grads[0]) + dot(upper, grads[1])
    depth = weight_term.shape[0]
    terms_ref[0:depth, :] = weight_term.astype(BF16)
    bias_term = jnp.sum(grad_pre, axis=0, keepdims=True)
    terms_ref[depth:, :] = jnp.broadcast_to(bias_term, (16, bias_term.shape[1])).astype(BF16)


def terms_of(hidden, grad_pre):
    return pl.pallas_call(
        terms_kernel,
        out_shape=jax.ShapeDtypeStruct((hidden.shape[1] + 16, grad_pre.shape[1]), BF16),
        compiler_params=params(),
        name="weight_terms",
    )(hidden, grad_pre)


def tree_sum(values):
    while len(values) > 1:
        values = [left + right for left, right in zip(values[::2], values[1::2])] + (
            values[-1:] if len(values) % 2 else []
        )
    return values[0]


def sum_kernel(*refs):
    refs[-1][...] = tree_sum([ref[...].astype(F32) for ref in refs[:-1]]).astype(BF16)


def sum_terms(items):
    return pl.pallas_call(
        sum_kernel,
        out_shape=jax.ShapeDtypeStruct(items[0].shape, BF16),
        compiler_params=params(),
        name="sum_terms",
    )(*items)


def stack_kernel(low, *refs):
    items, out_ref = refs[:-1], refs[-1]
    _, line, _ = spot(low)
    for step, item in enumerate(items):
        out_ref[source(line, step, len(items))] = item[...]


def stack_line(low, items):
    return pl.pallas_call(
        functools.partial(stack_kernel, low),
        out_shape=jax.ShapeDtypeStruct((len(items),) + items[0].shape, BF16),
        in_specs=[pl.BlockSpec(memory_space=pltpu.VMEM)] * len(items),
        compiler_params=params(),
        name="stack_line",
    )(*items)


def backward_kernel(steps, pieces, has_totals, dense_ref, *refs):
    stacks, inputs, outs = refs[: len(steps)], refs[len(steps) : -pieces], refs[-pieces:]
    terms = inputs[pieces if has_totals else 0 :]
    high, low, nodes, _ = dense_ref.shape
    row, _, plane = spot(low)
    for piece in range(pieces):
        columns = piece_columns(other(row, piece, pieces), nodes)
        total = inputs[piece][...] if has_totals else None
        for step, stack_ref in zip(steps, stacks):
            origin = source(plane, step, low)
            for chunk in range(high):
                term = dot(stack_ref[chunk], dense_ref[chunk, origin, :, columns])
                total = term if total is None else total + term
        depth = total.shape[0]
        outs[piece][0:depth, :] = total.astype(outs[piece].dtype)
        if terms and piece:
            outs[piece][depth:, :] = tree_sum([ref[...].astype(F32) for ref in terms]).astype(BF16)


def backward(dense, stacks, totals, terms=()):
    nodes, slots = dense.shape[2:]
    pieces = slots // nodes
    depth = next(iter(stacks.values())).shape[1]
    inputs = list(stacks.values()) + list(totals) + list(terms)

    def shape_of(piece):
        if terms and piece:
            return jax.ShapeDtypeStruct((depth + terms[0].shape[0], nodes), BF16)
        return jax.ShapeDtypeStruct((depth, nodes), F32)

    return pl.pallas_call(
        functools.partial(backward_kernel, tuple(stacks), pieces, bool(totals)),
        out_shape=[shape_of(piece) for piece in range(pieces)],
        in_specs=[pl.BlockSpec(memory_space=pltpu.VMEM)] * (1 + len(inputs)),
        compiler_params=params(),
        name="backward_product",
    )(dense, *inputs)


def finish_kernel(pieces, degrees_ref, own_ref, sent_ref, *refs):
    shares, outs = refs[: pieces - 1], refs[pieces - 1 :]
    total = own_ref[...]
    depth = total.shape[0]
    for share in shares:
        total = total + share[0:depth, :].astype(F32)
    row = lax.rsqrt(degrees_ref[...].astype(F32))
    outs[0][...] = jnp.transpose(row * total).astype(BF16)
    terms = tree_sum([ref[depth:, :].astype(F32) for ref in (sent_ref, *shares)])
    outs[1][...] = terms[0:depth]
    outs[2][...] = terms[depth : depth + 1]


def finish(degrees_row, own, sent, shares):
    depth, nodes = own.shape
    width = sent.shape[1]
    return pl.pallas_call(
        functools.partial(finish_kernel, len(shares) + 1),
        out_shape=[
            jax.ShapeDtypeStruct((nodes, depth), BF16),
            jax.ShapeDtypeStruct((depth, width), F32),
            jax.ShapeDtypeStruct((1, width), F32),
        ],
        compiler_params=params(),
        name="finish",
    )(degrees_row, own, sent, *shares)


def far_first(size):
    return range(size - 1, 0, -1)


def per_device(
    features, weight, bias_vector, cotangent, degrees, adjacency_tiles, tile_positions, tile_counts
):
    rows = lax.axis_size("row")
    cols = lax.axis_size("col")
    nodes = features.shape[0]
    per_part = nodes // BLOCK
    row_slots = cols * per_part
    col_slots = rows * per_part
    low = 4 if cols % 4 == 0 else 1
    high = cols // low

    degrees_row = degrees[None, :]

    def over_row(values, step):
        pairs = [(index, other(index, step, rows)) for index in range(rows)]
        return lax.ppermute(values, "row", pairs)

    def over_plane(values, step):
        pairs = [
            (index, index // low * low + other(index % low, step, low)) for index in range(cols)
        ]
        return lax.ppermute(values, "col", pairs)

    def over_line(values, step):
        pairs = [
            (index, other(index // low, step, high) * low + index % low) for index in range(cols)
        ]
        return lax.ppermute(values, "col", pairs)

    steps = range(1, rows)
    degrees_all = [degrees] + [over_row(degrees, step) for step in steps]
    features_all = [features] + [over_row(features, step) for step in steps]
    dense = densify(
        tile_positions, tile_counts, adjacency_tiles[0, 0], row_slots, col_slots
    ).reshape(high, low, nodes, col_slots * BLOCK)

    inputs = [values[None, :] for values in degrees_all] + features_all
    products, scaled = forward(dense, inputs, ((low - 1, True),), scaling=True)
    far_ones = tuple((step, True) for step in far_first(low - 1))
    rest = ((0, True),) + tuple((step, False) for step in (*far_first(low), 0))
    for wanted in (far_ones, rest):
        if wanted:
            products |= forward(dense, scaled, wanted)[0]
    onward = [products[0, True]] + [over_plane(products[step, True], step) for step in far_first(low)]
    here = [products[0, False]] + [over_plane(products[step, False], step) for step in far_first(low)]
    chunks = combine(onward)
    shares = [over_line(chunks[hop - 1], hop) for hop in far_first(high)]
    outgoing, hidden, preact, grad_pre = layer(here + shares, degrees_row, weight, bias_vector[None, :], cotangent)

    line = {0: outgoing} | {step: over_line(outgoing, step) for step in far_first(high)}
    terms = terms_of(hidden, grad_pre)
    activations = activations_of(preact)
    parts = {0: terms} | {step: over_plane(terms, step) for step in far_first(low)}
    line, parts = lax.optimization_barrier((line, parts))
    stacked = stack_line(low, [line[step] for step in range(high)])
    terms = sum_terms([parts[step] for step in range(low)])
    stacks = {0: stacked} | {step: over_plane(stacked, step) for step in far_first(low)}
    parts = {0: terms} | {step: over_line(terms, step) for step in far_first(high)}
    terms = [parts[step] for step in range(high)]
    steps, totals = list(stacks), []
    for group in (steps[: low // 2], steps[low // 2 :]):
        if group:
            arrived = {step: stacks[step] for step in group}
            totals = backward(dense, arrived, totals, terms if group[-1] == steps[-1] else ())
    returned = [over_row(totals[step], step) for step in range(1, rows)]
    grad_features, grad_weight, grad_bias = finish(degrees_row, totals[0], totals[1], returned)
    return activations, grad_features, grad_weight, grad_bias[0]


def solution(mesh):
    placed = (
        P(("row", "col"), None),
        P(),
        P(),
        P(("row", "col"), None),
        P(("row", "col")),
        P("row", "col", None, None, None),
        P("row", "col", None),
        P("row", "col"),
    )
    return jax.shard_map(
        per_device,
        mesh=mesh,
        in_specs=placed,
        out_specs=(P(("row", "col"), None), P(("row", "col"), None), P(), P()),
        check_vma=False,
    )
```

```python
import functools

import jax
import jax.numpy as jnp
from jax import lax
from jax.experimental import pallas as pl
from jax.experimental.pallas import tpu as pltpu
from jax.sharding import PartitionSpec as P

BLOCK = 128
VMEM_BYTES = 48 * 1024 * 1024
F32 = jnp.float32
BF16 = jnp.bfloat16


def other(index, step, size):
    if size & (size - 1) == 0:
        return index ^ step
    return (index + step) % size


def source(index, step, size):
    if size & (size - 1) == 0:
        return index ^ step
    return (index - step) % size


def params():
    return pltpu.CompilerParams(vmem_limit_bytes=VMEM_BYTES)


def in_hbm(values):
    return pltpu.with_memory_space_constraint(values, pltpu.HBM)


def dot(left, right, contract=((1,), (0,))):
    return lax.dot_general(left, right, (contract, ((), ())), preferred_element_type=F32)


def split_two(values):
    upper = values.astype(BF16)
    return upper, (values - upper.astype(F32)).astype(BF16)


def scale_columns(degrees_row, columns):
    row = lax.rsqrt(degrees_row.astype(F32))
    return row, jnp.transpose(jnp.broadcast_to(row, (columns, row.shape[1])))


def densify_kernel(
    col_slots, positions_hbm, counts_ref, tiles_ref, out_ref, positions_ref, taken_ref, zero_ref, sems
):
    places = taken_ref.shape[0]
    live = counts_ref[0, 0]
    fetch = pltpu.make_async_copy(positions_hbm, positions_ref, sems.at[0])
    fetch.start()
    zero_ref[...] = jnp.zeros_like(zero_ref)

    def clear(place, carry):
        taken_ref[place] = 0
        return carry

    lax.fori_loop(0, places, clear, 0, unroll=8)
    fetch.wait()

    def target(place):
        if col_slots & (col_slots - 1) == 0:
            row = lax.shift_right_logical(place, col_slots.bit_length() - 1)
            column = place & (col_slots - 1)
        else:
            row, column = lax.div(place, col_slots), lax.rem(place, col_slots)
        return out_ref.at[row, :, pl.ds(pl.multiple_of(column * BLOCK, BLOCK), BLOCK)]

    def send(slot):
        place = positions_ref[0, 0, slot]
        taken_ref[place] = 1
        pltpu.make_async_copy(tiles_ref.at[slot], target(place), sems.at[1]).start()

    def send_many(group, carry):
        for step in range(8):
            send(group * 8 + step)
        return carry

    def send_one(slot, carry):
        send(slot)
        return carry

    groups = lax.shift_right_logical(live, 3)
    lax.fori_loop(0, groups, send_many, 0)
    lax.fori_loop(groups * 8, live, send_one, 0)

    def blank(place, carry):
        @pl.when(taken_ref[place] == 0)
        def _():
            pltpu.make_async_copy(zero_ref, target(place), sems.at[1]).start()

        return carry

    @pl.when(live < places)
    def _():
        lax.fori_loop(0, places, blank, 0, unroll=8)

    pltpu.make_async_copy(out_ref, out_ref, sems.at[1]).wait()


def densify(positions, counts, tiles, row_slots, col_slots):
    return pl.pallas_call(
        functools.partial(densify_kernel, col_slots),
        out_shape=jax.ShapeDtypeStruct((row_slots, BLOCK, col_slots * BLOCK), BF16),
        in_specs=[
            pl.BlockSpec(memory_space=pltpu.HBM),
            pl.BlockSpec(memory_space=pltpu.SMEM),
            pl.BlockSpec(memory_space=pltpu.HBM),
        ],
        out_specs=pl.BlockSpec(memory_space=pl.ANY),
        scratch_shapes=[
            pltpu.SMEM(positions.shape, jnp.int32),
            pltpu.SMEM((row_slots * col_slots,), jnp.int32),
            pltpu.VMEM((BLOCK, BLOCK), BF16),
            pltpu.SemaphoreType.DMA((2,)),
        ],
        compiler_params=params(),
        name="densify",
    )(in_hbm(positions), counts, tiles)


def spot(low):
    col = lax.axis_index("col")
    if low & (low - 1) == 0:
        return lax.axis_index("row"), lax.shift_right_logical(col, low.bit_length() - 1), col & (low - 1)
    return lax.axis_index("row"), lax.div(col, low), lax.rem(col, low)


def piece_columns(index, nodes):
    return pl.ds(pl.multiple_of(index * nodes, nodes), nodes)


def forward_kernel(wanted, pieces, scaling, dense_ref, *refs):
    inputs = refs[: 2 * pieces if scaling else pieces]
    outs = refs[len(inputs) :]
    high, low, nodes, _ = dense_ref.shape
    row, line, plane = spot(low)
    if scaling:
        scaled = outs[len(wanted) :]
        for degrees_ref, features_ref, out_ref in zip(inputs[:pieces], inputs[pieces:], scaled):
            _, scale = scale_columns(degrees_ref[...], features_ref.shape[1])
            out_ref[...] = (scale * features_ref[...].astype(F32)).astype(BF16)
    else:
        scaled = inputs

    def product(step, hop):
        column, chunk = other(plane, step, low), other(line, hop, high)
        total = None
        for piece in range(pieces):
            columns = piece_columns(source(row, piece, pieces), nodes)
            term = dot(dense_ref[chunk, column, :, columns], scaled[piece][...])
            total = term if total is None else total + term
        return total

    for (step, onward), out_ref in zip(wanted, outs):
        if onward:
            for hop in far_first(high):
                out_ref[hop - 1] = product(step, hop).astype(out_ref.dtype)
        else:
            out_ref[...] = product(step, 0).astype(out_ref.dtype)


def forward(dense, inputs, wanted, scaling=False):
    high, _, nodes, _ = dense.shape
    pieces = len(inputs) // 2 if scaling else len(inputs)
    width = inputs[-1].shape[1]

    def shape_of(step, onward):
        shape = (high - 1, nodes, width) if onward else (nodes, width)
        return jax.ShapeDtypeStruct(shape, BF16 if step else F32)

    outs = pl.pallas_call(
        functools.partial(forward_kernel, wanted, pieces, scaling),
        out_shape=[shape_of(*item) for item in wanted]
        + [jax.ShapeDtypeStruct((nodes, width), BF16)] * (pieces if scaling else 0),
        in_specs=[pl.BlockSpec(memory_space=pltpu.VMEM)] * (1 + len(inputs)),
        compiler_params=params(),
        name="forward_product",
    )(dense, *inputs)
    return dict(zip(wanted, outs)), outs[len(wanted) :]


def combine_kernel(count, *refs):
    arrays, outs = refs[:count], refs[count:]
    for hop, out_ref in enumerate(outs):
        out_ref[...] = tree_sum([array[hop].astype(F32) for array in arrays]).astype(out_ref.dtype)


def combine(arrays):
    hops, nodes, columns = arrays[0].shape
    return pl.pallas_call(
        functools.partial(combine_kernel, len(arrays)),
        out_shape=[jax.ShapeDtypeStruct((nodes, columns), BF16)] * hops,
        in_specs=[pl.BlockSpec(memory_space=pltpu.VMEM)] * len(arrays),
        compiler_params=params(),
        name="combine",
    )(*arrays)


def layer_kernel(count, *refs):
    degrees_ref, weight_ref, bias_ref, cotangent_ref = refs[count : count + 4]
    outgoing_ref, hidden_ref, preact_ref, grad_pre_ref = refs[count + 4 :]
    total = tree_sum([ref[...].astype(F32) for ref in refs[:count]])
    row, scale = scale_columns(degrees_ref[...], total.shape[1])
    hidden = scale * total
    weight = weight_ref[...]
    upper, lower = split_two(hidden)
    preact = dot(upper, weight) + dot(lower, weight) + bias_ref[...]
    logistic = 1.0 / (1.0 + jnp.exp(-preact))
    grad_pre = cotangent_ref[...].astype(F32) * logistic * (1.0 + preact * (1.0 - logistic))
    upper, lower = split_two(grad_pre)
    across = ((1,), (1,))
    back = dot(weight, upper, across) + dot(weight, lower, across)
    outgoing_ref[...] = (row * back).astype(BF16)
    hidden_ref[...] = hidden
    preact_ref[...] = preact
    grad_pre_ref[...] = grad_pre


def layer(shares, degrees_row, weight, bias_row, cotangent):
    nodes = degrees_row.shape[1]
    depth, width = weight.shape
    return pl.pallas_call(
        functools.partial(layer_kernel, len(shares)),
        out_shape=[
            jax.ShapeDtypeStruct((depth, nodes), BF16),
            jax.ShapeDtypeStruct((nodes, depth), F32),
            jax.ShapeDtypeStruct((nodes, width), F32),
            jax.ShapeDtypeStruct((nodes, width), F32),
        ],
        compiler_params=params(),
        name="layer",
    )(*shares, degrees_row, weight, bias_row, cotangent)


def activations_kernel(preact_ref, out_ref):
    preact = preact_ref[...]
    out_ref[...] = (preact / (1.0 + jnp.exp(-preact))).astype(BF16)


def activations_of(preact):
    return pl.pallas_call(
        activations_kernel,
        out_shape=jax.ShapeDtypeStruct(preact.shape, BF16),
        compiler_params=params(),
        name="activations",
    )(preact)


def terms_kernel(hidden_ref, grad_pre_ref, *refs):
    outs, terms_ref = refs[:-1], refs[-1]
    grad_pre = grad_pre_ref[...]
    grads = split_two(grad_pre)
    upper, lower = split_two(jnp.transpose(hidden_ref[...]))
    terms_ref[...] = dot(upper, grads[0]) + dot(lower, grads[0]) + dot(upper, grads[1])
    bias_term = jnp.sum(grad_pre, axis=0, keepdims=True)
    pieces = len(outs)
    rows = terms_ref.shape[0] // pieces
    for step, out_ref in enumerate(outs):
        start = pl.multiple_of(other(lax.axis_index("row"), step, pieces) * rows, 8)
        out_ref[0:rows, :] = terms_ref[pl.ds(start, rows), :]
        out_ref[rows:, :] = jnp.broadcast_to(bias_term, (16, bias_term.shape[1]))


def terms_of(hidden, grad_pre):
    pieces = lax.axis_size("row")
    depth, width = hidden.shape[1], grad_pre.shape[1]
    return pl.pallas_call(
        terms_kernel,
        out_shape=[jax.ShapeDtypeStruct((depth // pieces + 16, width), F32)] * pieces,
        scratch_shapes=[pltpu.VMEM((depth, width), F32)],
        compiler_params=params(),
        name="weight_terms",
    )(hidden, grad_pre)


def pack_kernel(outgoing_ref, *refs):
    pieces, out_ref = refs[:-1], refs[-1]
    depth = outgoing_ref.shape[0]
    out_ref[0:depth, :] = outgoing_ref[...]
    out_ref[depth:, :] = tree_sum([piece[...] for piece in pieces]).astype(BF16)


def pack(outgoing, pieces):
    depth, nodes = outgoing.shape
    return pl.pallas_call(
        pack_kernel,
        out_shape=jax.ShapeDtypeStruct((depth + pieces[0].shape[0], nodes), BF16),
        compiler_params=params(),
        name="pack",
    )(outgoing, *pieces)


def tree_sum(values):
    while len(values) > 1:
        values = [left + right for left, right in zip(values[::2], values[1::2])] + (
            values[-1:] if len(values) % 2 else []
        )
    return values[0]


def sum_kernel(depth, *refs):
    refs[-1][...] = tree_sum([ref[depth:, :].astype(F32) for ref in refs[:-1]]).astype(BF16)


def sum_terms(parcels, depth):
    rows, width = parcels[0].shape
    return pl.pallas_call(
        functools.partial(sum_kernel, depth),
        out_shape=jax.ShapeDtypeStruct((rows - depth, width), BF16),
        compiler_params=params(),
        name="sum_terms",
    )(*parcels)


def stack_kernel(*refs):
    for step, ref in enumerate(refs[:-1]):
        refs[-1][step] = ref[...]


def stack_line(items):
    return pl.pallas_call(
        stack_kernel,
        out_shape=jax.ShapeDtypeStruct((len(items),) + items[0].shape, BF16),
        compiler_params=params(),
        name="stack_line",
    )(*items)


def backward_kernel(steps, pieces, has_totals, dense_ref, *refs):
    count = len(steps)
    parcels, stacks = refs[:count], refs[count : 2 * count]
    inputs, outs = refs[2 * count : -pieces], refs[-pieces:]
    terms = inputs[pieces if has_totals else 0 :]
    high, low, nodes, _ = dense_ref.shape
    row, line, plane = spot(low)
    for piece in range(pieces):
        columns = piece_columns(other(row, piece, pieces), nodes)
        total = inputs[piece][...] if has_totals else None
        for step, parcel_ref, stack_ref in zip(steps, parcels, stacks):
            origin = source(plane, step, low)
            depth = stack_ref.shape[1]
            for hop in range(high):
                values = stack_ref[hop - 1] if hop else parcel_ref[0:depth, :]
                term = dot(values, dense_ref[source(line, hop, high), origin, :, columns])
                total = term if total is None else total + term
        outs[piece][0:depth, :] = total.astype(outs[piece].dtype)
        if terms and piece:
            outs[piece][depth:, :] = tree_sum([ref[...].astype(F32) for ref in terms]).astype(BF16)


def backward(dense, parcels, stacks, totals, terms=()):
    nodes, slots = dense.shape[2:]
    pieces = slots // nodes
    depth = next(iter(stacks.values())).shape[1]
    inputs = list(parcels.values()) + list(stacks.values()) + list(totals) + list(terms)

    def shape_of(piece):
        if terms and piece:
            return jax.ShapeDtypeStruct((depth + terms[0].shape[0], nodes), BF16)
        return jax.ShapeDtypeStruct((depth, nodes), F32)

    return pl.pallas_call(
        functools.partial(backward_kernel, tuple(stacks), pieces, bool(totals)),
        out_shape=[shape_of(piece) for piece in range(pieces)],
        in_specs=[pl.BlockSpec(memory_space=pltpu.VMEM)] * (1 + len(inputs)),
        compiler_params=params(),
        name="backward_product",
    )(dense, *inputs)


def finish_kernel(pieces, degrees_ref, own_ref, sent_ref, *refs):
    shares, outs = refs[: pieces - 1], refs[pieces - 1 :]
    total = own_ref[...]
    depth = total.shape[0]
    for share in shares:
        total = total + share[0:depth, :].astype(F32)
    row = lax.rsqrt(degrees_ref[...].astype(F32))
    outs[0][...] = jnp.transpose(row * total).astype(BF16)
    rows = depth // pieces
    for step, ref in enumerate((sent_ref, *shares)):
        start = pl.multiple_of(source(lax.axis_index("row"), step, pieces) * rows, 8)
        outs[1][pl.ds(start, rows), :] = ref[depth : depth + rows, :].astype(F32)
    outs[2][...] = sent_ref[depth + rows : depth + rows + 16, :].astype(F32)[0:1]


def finish(degrees_row, own, sent, shares):
    depth, nodes = own.shape
    width = sent.shape[1]
    return pl.pallas_call(
        functools.partial(finish_kernel, len(shares) + 1),
        out_shape=[
            jax.ShapeDtypeStruct((nodes, depth), BF16),
            jax.ShapeDtypeStruct((depth, width), F32),
            jax.ShapeDtypeStruct((1, width), F32),
        ],
        compiler_params=params(),
        name="finish",
    )(degrees_row, own, sent, *shares)


def far_first(size):
    return range(size - 1, 0, -1)


def per_device(
    features, weight, bias_vector, cotangent, degrees, adjacency_tiles, tile_positions, tile_counts
):
    rows = lax.axis_size("row")
    cols = lax.axis_size("col")
    nodes = features.shape[0]
    per_part = nodes // BLOCK
    row_slots = cols * per_part
    col_slots = rows * per_part
    low = 4 if cols % 4 == 0 else 1
    high = cols // low

    degrees_row = degrees[None, :]

    def over_row(values, step):
        pairs = [(index, other(index, step, rows)) for index in range(rows)]
        return lax.ppermute(values, "row", pairs)

    def over_plane(values, step):
        pairs = [
            (index, index // low * low + other(index % low, step, low)) for index in range(cols)
        ]
        return lax.ppermute(values, "col", pairs)

    def over_line(values, step):
        pairs = [
            (index, other(index // low, step, high) * low + index % low) for index in range(cols)
        ]
        return lax.ppermute(values, "col", pairs)

    steps = range(1, rows)
    degrees_all = [degrees] + [over_row(degrees, step) for step in steps]
    features_all = [features] + [over_row(features, step) for step in steps]
    dense = densify(
        tile_positions, tile_counts, adjacency_tiles[0, 0], row_slots, col_slots
    ).reshape(high, low, nodes, col_slots * BLOCK)

    inputs = [values[None, :] for values in degrees_all] + features_all
    products, scaled = forward(dense, inputs, ((low - 1, True),), scaling=True)
    far_ones = tuple((step, True) for step in far_first(low - 1))
    rest = ((0, True),) + tuple((step, False) for step in (*far_first(low), 0))
    for wanted in (far_ones, rest):
        if wanted:
            products |= forward(dense, scaled, wanted)[0]
    onward = [products[0, True]] + [over_plane(products[step, True], step) for step in far_first(low)]
    here = [products[0, False]] + [over_plane(products[step, False], step) for step in far_first(low)]
    chunks = combine(onward)
    shares = [over_line(chunks[hop - 1], hop) for hop in far_first(high)]
    outgoing, hidden, preact, grad_pre = layer(here + shares, degrees_row, weight, bias_vector[None, :], cotangent)

    line = [over_line(outgoing, step) for step in far_first(high)][::-1]
    pieces = terms_of(hidden, grad_pre)
    activations = activations_of(preact)
    parcel = pack(outgoing, [pieces[0]] + [over_row(pieces[step], step) for step in range(1, rows)])
    parcels = {0: parcel} | {step: over_plane(parcel, step) for step in far_first(low)}
    line, parcels = lax.optimization_barrier((line, parcels))
    stacked = stack_line(line)
    stacks = {0: stacked} | {step: over_plane(stacked, step) for step in far_first(low)}
    terms = sum_terms([parcels[step] for step in range(low)], weight.shape[0])
    parts = {0: terms} | {step: over_line(terms, step) for step in far_first(high)}
    terms = [parts[step] for step in range(high)]
    steps, totals = list(stacks), []
    for group in (steps[: low // 2], steps[low // 2 :]):
        if group:
            totals = backward(
                dense,
                {step: parcels[step] for step in group},
                {step: stacks[step] for step in group},
                totals,
                terms if group[-1] == steps[-1] else (),
            )
    returned = [over_row(totals[step], step) for step in range(1, rows)]
    grad_features, grad_weight, grad_bias = finish(degrees_row, totals[0], totals[1], returned)
    return activations, grad_features, grad_weight, grad_bias[0]


def solution(mesh):
    placed = (
        P(("row", "col"), None),
        P(),
        P(),
        P(("row", "col"), None),
        P(("row", "col")),
        P("row", "col", None, None, None),
        P("row", "col", None),
        P("row", "col"),
    )
    return jax.shard_map(
        per_device,
        mesh=mesh,
        in_specs=placed,
        out_specs=(P(("row", "col"), None), P(("row", "col"), None), P(), P()),
        check_vma=False,
    )
```

```python
import functools

import jax
import jax.numpy as jnp
from jax import lax
from jax.experimental import pallas as pl
from jax.experimental.pallas import tpu as pltpu
from jax.sharding import PartitionSpec as P

BLOCK = 128
VMEM_BYTES = 48 * 1024 * 1024
F32 = jnp.float32
BF16 = jnp.bfloat16


def other(index, step, size):
    if size & (size - 1) == 0:
        return index ^ step
    return (index + step) % size


def source(index, step, size):
    if size & (size - 1) == 0:
        return index ^ step
    return (index - step) % size


def params():
    return pltpu.CompilerParams(vmem_limit_bytes=VMEM_BYTES)


def in_hbm(values):
    return pltpu.with_memory_space_constraint(values, pltpu.HBM)


def dot(left, right, contract=((1,), (0,))):
    return lax.dot_general(left, right, (contract, ((), ())), preferred_element_type=F32)


def split_two(values):
    upper = values.astype(BF16)
    return upper, (values - upper.astype(F32)).astype(BF16)


def scale_columns(degrees_row, columns):
    row = lax.rsqrt(degrees_row.astype(F32))
    return row, jnp.transpose(jnp.broadcast_to(row, (columns, row.shape[1])))


def densify_kernel(
    col_slots, positions_hbm, counts_ref, tiles_ref, out_ref, positions_ref, taken_ref, zero_ref, sems
):
    places = taken_ref.shape[0]
    live = counts_ref[0, 0]
    fetch = pltpu.make_async_copy(positions_hbm, positions_ref, sems.at[0])
    fetch.start()
    zero_ref[...] = jnp.zeros_like(zero_ref)

    def clear(place, carry):
        taken_ref[place] = 0
        return carry

    lax.fori_loop(0, places, clear, 0, unroll=8)
    fetch.wait()

    def target(place):
        if col_slots & (col_slots - 1) == 0:
            row = lax.shift_right_logical(place, col_slots.bit_length() - 1)
            column = place & (col_slots - 1)
        else:
            row, column = lax.div(place, col_slots), lax.rem(place, col_slots)
        return out_ref.at[row, :, pl.ds(pl.multiple_of(column * BLOCK, BLOCK), BLOCK)]

    def send(slot):
        place = positions_ref[0, 0, slot]
        taken_ref[place] = 1
        pltpu.make_async_copy(tiles_ref.at[slot], target(place), sems.at[1]).start()

    def send_many(group, carry):
        for step in range(8):
            send(group * 8 + step)
        return carry

    def send_one(slot, carry):
        send(slot)
        return carry

    groups = lax.shift_right_logical(live, 3)
    lax.fori_loop(0, groups, send_many, 0)
    lax.fori_loop(groups * 8, live, send_one, 0)

    def blank(place, carry):
        @pl.when(taken_ref[place] == 0)
        def _():
            pltpu.make_async_copy(zero_ref, target(place), sems.at[1]).start()

        return carry

    @pl.when(live < places)
    def _():
        lax.fori_loop(0, places, blank, 0, unroll=8)

    pltpu.make_async_copy(out_ref, out_ref, sems.at[1]).wait()


def densify(positions, counts, tiles, row_slots, col_slots):
    return pl.pallas_call(
        functools.partial(densify_kernel, col_slots),
        out_shape=jax.ShapeDtypeStruct((row_slots, BLOCK, col_slots * BLOCK), BF16),
        in_specs=[
            pl.BlockSpec(memory_space=pltpu.HBM),
            pl.BlockSpec(memory_space=pltpu.SMEM),
            pl.BlockSpec(memory_space=pltpu.HBM),
        ],
        out_specs=pl.BlockSpec(memory_space=pl.ANY),
        scratch_shapes=[
            pltpu.SMEM(positions.shape, jnp.int32),
            pltpu.SMEM((row_slots * col_slots,), jnp.int32),
            pltpu.VMEM((BLOCK, BLOCK), BF16),
            pltpu.SemaphoreType.DMA((2,)),
        ],
        compiler_params=params(),
        name="densify",
    )(in_hbm(positions), counts, tiles)


def spot(low):
    col = lax.axis_index("col")
    if low & (low - 1) == 0:
        return lax.axis_index("row"), lax.shift_right_logical(col, low.bit_length() - 1), col & (low - 1)
    return lax.axis_index("row"), lax.div(col, low), lax.rem(col, low)


def piece_columns(index, nodes):
    return pl.ds(pl.multiple_of(index * nodes, nodes), nodes)


def forward_kernel(wanted, pieces, scaling, dense_ref, *refs):
    inputs = refs[: 2 * pieces if scaling else pieces]
    outs = refs[len(inputs) :]
    high, low, nodes, _ = dense_ref.shape
    row, line, plane = spot(low)
    if scaling:
        scaled = outs[len(wanted) :]
        for degrees_ref, features_ref, out_ref in zip(inputs[:pieces], inputs[pieces:], scaled):
            _, scale = scale_columns(degrees_ref[...], features_ref.shape[1])
            out_ref[...] = (scale * features_ref[...].astype(F32)).astype(BF16)
    else:
        scaled = inputs

    def product(step, hop):
        column, chunk = other(plane, step, low), other(line, hop, high)
        total = None
        for piece in range(pieces):
            columns = piece_columns(source(row, piece, pieces), nodes)
            term = dot(dense_ref[chunk, column, :, columns], scaled[piece][...])
            total = term if total is None else total + term
        return total

    for (step, onward), out_ref in zip(wanted, outs):
        if onward:
            for hop in far_first(high):
                out_ref[hop - 1] = product(step, hop).astype(out_ref.dtype)
        else:
            out_ref[...] = product(step, 0).astype(out_ref.dtype)


def forward(dense, inputs, wanted, scaling=False):
    high, _, nodes, _ = dense.shape
    pieces = len(inputs) // 2 if scaling else len(inputs)
    width = inputs[-1].shape[1]

    def shape_of(step, onward):
        shape = (high - 1, nodes, width) if onward else (nodes, width)
        return jax.ShapeDtypeStruct(shape, BF16 if step else F32)

    outs = pl.pallas_call(
        functools.partial(forward_kernel, wanted, pieces, scaling),
        out_shape=[shape_of(*item) for item in wanted]
        + [jax.ShapeDtypeStruct((nodes, width), BF16)] * (pieces if scaling else 0),
        in_specs=[pl.BlockSpec(memory_space=pltpu.VMEM)] * (1 + len(inputs)),
        compiler_params=params(),
        name="forward_product",
    )(dense, *inputs)
    return dict(zip(wanted, outs)), outs[len(wanted) :]


def combine_kernel(count, *refs):
    arrays, outs = refs[:count], refs[count:]
    for hop, out_ref in enumerate(outs):
        out_ref[...] = tree_sum([array[hop].astype(F32) for array in arrays]).astype(out_ref.dtype)


def combine(arrays):
    hops, nodes, columns = arrays[0].shape
    return pl.pallas_call(
        functools.partial(combine_kernel, len(arrays)),
        out_shape=[jax.ShapeDtypeStruct((nodes, columns), BF16)] * hops,
        in_specs=[pl.BlockSpec(memory_space=pltpu.VMEM)] * len(arrays),
        compiler_params=params(),
        name="combine",
    )(*arrays)


def layer_kernel(count, *refs):
    degrees_ref, weight_ref, bias_ref, cotangent_ref = refs[count : count + 4]
    outgoing_ref, hidden_ref, preact_ref, grad_pre_ref = refs[count + 4 :]
    total = tree_sum([ref[...].astype(F32) for ref in refs[:count]])
    row, scale = scale_columns(degrees_ref[...], total.shape[1])
    hidden = scale * total
    weight = weight_ref[...]
    upper, lower = split_two(hidden)
    preact = dot(upper, weight) + dot(lower, weight) + bias_ref[...]
    logistic = 1.0 / (1.0 + jnp.exp(-preact))
    grad_pre = cotangent_ref[...].astype(F32) * logistic * (1.0 + preact * (1.0 - logistic))
    upper, lower = split_two(grad_pre)
    across = ((1,), (1,))
    back = dot(weight, upper, across) + dot(weight, lower, across)
    outgoing_ref[...] = (row * back).astype(BF16)
    hidden_ref[...] = hidden
    preact_ref[...] = preact
    grad_pre_ref[...] = grad_pre


def layer(shares, degrees_row, weight, bias_row, cotangent):
    nodes = degrees_row.shape[1]
    depth, width = weight.shape
    return pl.pallas_call(
        functools.partial(layer_kernel, len(shares)),
        out_shape=[
            jax.ShapeDtypeStruct((depth, nodes), BF16),
            jax.ShapeDtypeStruct((nodes, depth), F32),
            jax.ShapeDtypeStruct((nodes, width), F32),
            jax.ShapeDtypeStruct((nodes, width), F32),
        ],
        compiler_params=params(),
        name="layer",
    )(*shares, degrees_row, weight, bias_row, cotangent)


def activations_kernel(preact_ref, out_ref):
    preact = preact_ref[...]
    out_ref[...] = (preact / (1.0 + jnp.exp(-preact))).astype(BF16)


def activations_of(preact):
    return pl.pallas_call(
        activations_kernel,
        out_shape=jax.ShapeDtypeStruct(preact.shape, BF16),
        compiler_params=params(),
        name="activations",
    )(preact)


def terms_kernel(hidden_ref, grad_pre_ref, *refs):
    outs, terms_ref = refs[:-1], refs[-1]
    grad_pre = grad_pre_ref[...]
    grads = split_two(grad_pre)
    upper, lower = split_two(jnp.transpose(hidden_ref[...]))
    terms_ref[...] = dot(upper, grads[0]) + dot(lower, grads[0]) + dot(upper, grads[1])
    bias_term = jnp.sum(grad_pre, axis=0, keepdims=True)
    pieces = len(outs)
    rows = terms_ref.shape[0] // pieces
    for step, out_ref in enumerate(outs):
        start = pl.multiple_of(other(lax.axis_index("row"), step, pieces) * rows, 8)
        out_ref[0:rows, :] = terms_ref[pl.ds(start, rows), :]
        out_ref[rows:, :] = jnp.broadcast_to(bias_term, (16, bias_term.shape[1]))


def terms_of(hidden, grad_pre):
    pieces = lax.axis_size("row")
    depth, width = hidden.shape[1], grad_pre.shape[1]
    return pl.pallas_call(
        terms_kernel,
        out_shape=[jax.ShapeDtypeStruct((depth // pieces + 16, width), F32)] * pieces,
        scratch_shapes=[pltpu.VMEM((depth, width), F32)],
        compiler_params=params(),
        name="weight_terms",
    )(hidden, grad_pre)


def pack_kernel(outgoing_ref, *refs):
    pieces, out_ref = refs[:-1], refs[-1]
    depth = outgoing_ref.shape[0]
    out_ref[0:depth, :] = outgoing_ref[...]
    out_ref[depth:, :] = tree_sum([piece[...] for piece in pieces]).astype(BF16)


def pack(outgoing, pieces):
    depth, nodes = outgoing.shape
    return pl.pallas_call(
        pack_kernel,
        out_shape=jax.ShapeDtypeStruct((depth + pieces[0].shape[0], nodes), BF16),
        compiler_params=params(),
        name="pack",
    )(outgoing, *pieces)


def tree_sum(values):
    while len(values) > 1:
        values = [left + right for left, right in zip(values[::2], values[1::2])] + (
            values[-1:] if len(values) % 2 else []
        )
    return values[0]


def sum_kernel(depth, *refs):
    refs[-1][...] = tree_sum([ref[depth:, :].astype(F32) for ref in refs[:-1]]).astype(BF16)


def sum_terms(parcels, depth):
    rows, width = parcels[0].shape
    return pl.pallas_call(
        functools.partial(sum_kernel, depth),
        out_shape=jax.ShapeDtypeStruct((rows - depth, width), BF16),
        compiler_params=params(),
        name="sum_terms",
    )(*parcels)


def stack_kernel(*refs):
    for step, ref in enumerate(refs[:-1]):
        refs[-1][step] = ref[...]


def stack_line(items):
    return pl.pallas_call(
        stack_kernel,
        out_shape=jax.ShapeDtypeStruct((len(items),) + items[0].shape, BF16),
        compiler_params=params(),
        name="stack_line",
    )(*items)


def backward_kernel(steps, pieces, has_totals, dense_ref, *refs):
    count = len(steps)
    parcels, stacks = refs[:count], refs[count : 2 * count]
    inputs, outs = refs[2 * count : -pieces], refs[-pieces:]
    terms = inputs[pieces if has_totals else 0 :]
    high, low, nodes, _ = dense_ref.shape
    row, line, plane = spot(low)
    for piece in range(pieces):
        columns = piece_columns(other(row, piece, pieces), nodes)
        total = inputs[piece][...] if has_totals else None
        for step, parcel_ref, stack_ref in zip(steps, parcels, stacks):
            origin = source(plane, step, low)
            depth = stack_ref.shape[1]
            for hop in range(high):
                values = stack_ref[hop - 1] if hop else parcel_ref[0:depth, :]
                term = dot(values, dense_ref[source(line, hop, high), origin, :, columns])
                total = term if total is None else total + term
        outs[piece][0:depth, :] = total.astype(outs[piece].dtype)
        if terms and piece:
            outs[piece][depth:, :] = tree_sum([ref[...].astype(F32) for ref in terms]).astype(BF16)


def backward(dense, parcels, stacks, totals, terms=()):
    nodes, slots = dense.shape[2:]
    pieces = slots // nodes
    depth = next(iter(stacks.values())).shape[1]
    inputs = list(parcels.values()) + list(stacks.values()) + list(totals) + list(terms)

    def shape_of(piece):
        if terms and piece:
            return jax.ShapeDtypeStruct((depth + terms[0].shape[0], nodes), BF16)
        return jax.ShapeDtypeStruct((depth, nodes), F32)

    return pl.pallas_call(
        functools.partial(backward_kernel, tuple(stacks), pieces, bool(totals)),
        out_shape=[shape_of(piece) for piece in range(pieces)],
        in_specs=[pl.BlockSpec(memory_space=pltpu.VMEM)] * (1 + len(inputs)),
        compiler_params=params(),
        name="backward_product",
    )(dense, *inputs)


def finish_kernel(pieces, degrees_ref, own_ref, sent_ref, *refs):
    shares, outs = refs[: pieces - 1], refs[pieces - 1 :]
    total = own_ref[...]
    depth = total.shape[0]
    for share in shares:
        total = total + share[0:depth, :].astype(F32)
    row = lax.rsqrt(degrees_ref[...].astype(F32))
    outs[0][...] = jnp.transpose(row * total).astype(BF16)
    rows = depth // pieces
    for step, ref in enumerate((sent_ref, *shares)):
        start = pl.multiple_of(source(lax.axis_index("row"), step, pieces) * rows, 8)
        outs[1][pl.ds(start, rows), :] = ref[depth : depth + rows, :].astype(F32)
    outs[2][...] = sent_ref[depth + rows : depth + rows + 16, :].astype(F32)[0:1]


def finish(degrees_row, own, sent, shares):
    depth, nodes = own.shape
    width = sent.shape[1]
    return pl.pallas_call(
        functools.partial(finish_kernel, len(shares) + 1),
        out_shape=[
            jax.ShapeDtypeStruct((nodes, depth), BF16),
            jax.ShapeDtypeStruct((depth, width), F32),
            jax.ShapeDtypeStruct((1, width), F32),
        ],
        compiler_params=params(),
        name="finish",
    )(degrees_row, own, sent, *shares)


def far_first(size):
    return range(size - 1, 0, -1)


def per_device(
    features, weight, bias_vector, cotangent, degrees, adjacency_tiles, tile_positions, tile_counts
):
    rows = lax.axis_size("row")
    cols = lax.axis_size("col")
    nodes = features.shape[0]
    per_part = nodes // BLOCK
    row_slots = cols * per_part
    col_slots = rows * per_part
    low = 4 if cols % 4 == 0 else 1
    high = cols // low

    degrees_row = degrees[None, :]

    def over_row(values, step):
        pairs = [(index, other(index, step, rows)) for index in range(rows)]
        return lax.ppermute(values, "row", pairs)

    def over_plane(values, step):
        pairs = [
            (index, index // low * low + other(index % low, step, low)) for index in range(cols)
        ]
        return lax.ppermute(values, "col", pairs)

    def over_line(values, step):
        pairs = [
            (index, other(index // low, step, high) * low + index % low) for index in range(cols)
        ]
        return lax.ppermute(values, "col", pairs)

    steps = range(1, rows)
    degrees_all = [degrees] + [over_row(degrees, step) for step in steps]
    features_all = [features] + [over_row(features, step) for step in steps]
    dense = densify(
        tile_positions, tile_counts, adjacency_tiles[0, 0], row_slots, col_slots
    ).reshape(high, low, nodes, col_slots * BLOCK)

    inputs = [values[None, :] for values in degrees_all] + features_all
    products, scaled = forward(dense, inputs, ((low - 1, True),), scaling=True)
    far_ones = tuple((step, True) for step in far_first(low - 1))
    rest = ((0, True),) + tuple((step, False) for step in (*far_first(low), 0))
    if far_ones:
        products |= forward(dense, scaled, far_ones)[0]
    onward = [over_plane(products[step, True], step) for step in far_first(low)]
    scaled, onward[:1] = lax.optimization_barrier((scaled, onward[:1]))
    products |= forward(dense, scaled, rest)[0]
    onward = [products[0, True]] + onward
    here = [products[0, False]] + [over_plane(products[step, False], step) for step in far_first(low)]
    chunks = combine(onward)
    shares = [over_line(chunks[hop - 1], hop) for hop in far_first(high)]
    outgoing, hidden, preact, grad_pre = layer(here + shares, degrees_row, weight, bias_vector[None, :], cotangent)

    line = [over_line(outgoing, step) for step in far_first(high)][::-1]
    pieces = terms_of(hidden, grad_pre)
    activations = activations_of(preact)
    parcel = pack(outgoing, [pieces[0]] + [over_row(pieces[step], step) for step in range(1, rows)])
    parcels = {0: parcel} | {step: over_plane(parcel, step) for step in far_first(low)}
    stacked = stack_line(line)
    stacks = {0: stacked} | {step: over_plane(stacked, step) for step in far_first(low)}
    terms = sum_terms([parcels[step] for step in range(low)], weight.shape[0])
    parts = {0: terms} | {step: over_line(terms, step) for step in far_first(high)}
    terms = [parts[step] for step in range(high)]
    steps, totals = list(stacks), []
    for group in (steps[: low // 2], steps[low // 2 :]):
        if group:
            totals = backward(
                dense,
                {step: parcels[step] for step in group},
                {step: stacks[step] for step in group},
                totals,
                terms if group[-1] == steps[-1] else (),
            )
    returned = [over_row(totals[step], step) for step in range(1, rows)]
    grad_features, grad_weight, grad_bias = finish(degrees_row, totals[0], totals[1], returned)
    return activations, grad_features, grad_weight, grad_bias[0]


def solution(mesh):
    placed = (
        P(("row", "col"), None),
        P(),
        P(),
        P(("row", "col"), None),
        P(("row", "col")),
        P("row", "col", None, None, None),
        P("row", "col", None),
        P("row", "col"),
    )
    return jax.shard_map(
        per_device,
        mesh=mesh,
        in_specs=placed,
        out_specs=(P(("row", "col"), None), P(("row", "col"), None), P(), P()),
        check_vma=False,
    )
```

```python
import functools

import jax
import jax.numpy as jnp
from jax import lax
from jax.experimental import pallas as pl
from jax.experimental.pallas import tpu as pltpu
from jax.sharding import PartitionSpec as P

BLOCK = 128
VMEM_BYTES = 48 * 1024 * 1024
F32 = jnp.float32
BF16 = jnp.bfloat16


def other(index, step, size):
    if size & (size - 1) == 0:
        return index ^ step
    return (index + step) % size


def source(index, step, size):
    if size & (size - 1) == 0:
        return index ^ step
    return (index - step) % size


def params():
    return pltpu.CompilerParams(vmem_limit_bytes=VMEM_BYTES)


def in_hbm(values):
    return pltpu.with_memory_space_constraint(values, pltpu.HBM)


def dot(left, right, contract=((1,), (0,))):
    return lax.dot_general(left, right, (contract, ((), ())), preferred_element_type=F32)


def split_two(values):
    upper = values.astype(BF16)
    return upper, (values - upper.astype(F32)).astype(BF16)


def scale_columns(degrees_row, columns):
    row = lax.rsqrt(degrees_row.astype(F32))
    return row, jnp.transpose(jnp.broadcast_to(row, (columns, row.shape[1])))


def densify_kernel(
    col_slots, positions_hbm, counts_ref, tiles_ref, out_ref, positions_ref, taken_ref, zero_ref, sems
):
    places = taken_ref.shape[0]
    live = counts_ref[0, 0]
    fetch = pltpu.make_async_copy(positions_hbm, positions_ref, sems.at[0])
    fetch.start()
    zero_ref[...] = jnp.zeros_like(zero_ref)

    def clear(place, carry):
        taken_ref[place] = 0
        return carry

    lax.fori_loop(0, places, clear, 0, unroll=8)
    fetch.wait()

    def target(place):
        if col_slots & (col_slots - 1) == 0:
            row = lax.shift_right_logical(place, col_slots.bit_length() - 1)
            column = place & (col_slots - 1)
        else:
            row, column = lax.div(place, col_slots), lax.rem(place, col_slots)
        return out_ref.at[row, :, pl.ds(pl.multiple_of(column * BLOCK, BLOCK), BLOCK)]

    def send(slot):
        place = positions_ref[0, 0, slot]
        taken_ref[place] = 1
        pltpu.make_async_copy(tiles_ref.at[slot], target(place), sems.at[1]).start()

    def send_many(group, carry):
        for step in range(8):
            send(group * 8 + step)
        return carry

    def send_one(slot, carry):
        send(slot)
        return carry

    groups = lax.shift_right_logical(live, 3)
    lax.fori_loop(0, groups, send_many, 0)
    lax.fori_loop(groups * 8, live, send_one, 0)

    def blank(place, carry):
        @pl.when(taken_ref[place] == 0)
        def _():
            pltpu.make_async_copy(zero_ref, target(place), sems.at[1]).start()

        return carry

    @pl.when(live < places)
    def _():
        lax.fori_loop(0, places, blank, 0, unroll=8)

    pltpu.make_async_copy(out_ref, out_ref, sems.at[1]).wait()


def densify(positions, counts, tiles, row_slots, col_slots):
    return pl.pallas_call(
        functools.partial(densify_kernel, col_slots),
        out_shape=jax.ShapeDtypeStruct((row_slots, BLOCK, col_slots * BLOCK), BF16),
        in_specs=[
            pl.BlockSpec(memory_space=pltpu.HBM),
            pl.BlockSpec(memory_space=pltpu.SMEM),
            pl.BlockSpec(memory_space=pltpu.HBM),
        ],
        out_specs=pl.BlockSpec(memory_space=pl.ANY),
        scratch_shapes=[
            pltpu.SMEM(positions.shape, jnp.int32),
            pltpu.SMEM((row_slots * col_slots,), jnp.int32),
            pltpu.VMEM((BLOCK, BLOCK), BF16),
            pltpu.SemaphoreType.DMA((2,)),
        ],
        compiler_params=params(),
        name="densify",
    )(in_hbm(positions), counts, tiles)


def spot(low):
    col = lax.axis_index("col")
    if low & (low - 1) == 0:
        return lax.axis_index("row"), lax.shift_right_logical(col, low.bit_length() - 1), col & (low - 1)
    return lax.axis_index("row"), lax.div(col, low), lax.rem(col, low)


def piece_columns(index, nodes):
    return pl.ds(pl.multiple_of(index * nodes, nodes), nodes)


def forward_kernel(wanted, pieces, scaling, dense_ref, *refs):
    inputs = refs[: 2 * pieces if scaling else pieces]
    outs = refs[len(inputs) :]
    high, low, nodes, _ = dense_ref.shape
    row, line, plane = spot(low)
    if scaling:
        scaled = outs[len(wanted) :]
        for degrees_ref, features_ref, out_ref in zip(inputs[:pieces], inputs[pieces:], scaled):
            _, scale = scale_columns(degrees_ref[...], features_ref.shape[1])
            out_ref[...] = (scale * features_ref[...].astype(F32)).astype(BF16)
    else:
        scaled = inputs

    def product(step, hop):
        column, chunk = other(plane, step, low), other(line, hop, high)
        total = None
        for piece in range(pieces):
            columns = piece_columns(source(row, piece, pieces), nodes)
            term = dot(dense_ref[chunk, column, :, columns], scaled[piece][...])
            total = term if total is None else total + term
        return total

    for (step, onward), out_ref in zip(wanted, outs):
        if onward:
            for hop in far_first(high):
                out_ref[hop - 1] = product(step, hop).astype(out_ref.dtype)
        else:
            out_ref[...] = product(step, 0).astype(out_ref.dtype)


def forward(dense, inputs, wanted, scaling=False):
    high, _, nodes, _ = dense.shape
    pieces = len(inputs) // 2 if scaling else len(inputs)
    width = inputs[-1].shape[1]

    def shape_of(step, onward):
        shape = (high - 1, nodes, width) if onward else (nodes, width)
        return jax.ShapeDtypeStruct(shape, BF16 if step else F32)

    outs = pl.pallas_call(
        functools.partial(forward_kernel, wanted, pieces, scaling),
        out_shape=[shape_of(*item) for item in wanted]
        + [jax.ShapeDtypeStruct((nodes, width), BF16)] * (pieces if scaling else 0),
        in_specs=[pl.BlockSpec(memory_space=pltpu.VMEM)] * (1 + len(inputs)),
        compiler_params=params(),
        name="forward_product",
    )(dense, *inputs)
    return dict(zip(wanted, outs)), outs[len(wanted) :]


def combine_kernel(count, *refs):
    arrays, outs = refs[:count], refs[count:]
    for hop, out_ref in enumerate(outs):
        out_ref[...] = tree_sum([array[hop].astype(F32) for array in arrays]).astype(out_ref.dtype)


def combine(arrays):
    hops, nodes, columns = arrays[0].shape
    return pl.pallas_call(
        functools.partial(combine_kernel, len(arrays)),
        out_shape=[jax.ShapeDtypeStruct((nodes, columns), BF16)] * hops,
        in_specs=[pl.BlockSpec(memory_space=pltpu.VMEM)] * len(arrays),
        compiler_params=params(),
        name="combine",
    )(*arrays)


def layer_kernel(count, *refs):
    degrees_ref, weight_ref, bias_ref, cotangent_ref = refs[count : count + 4]
    outgoing_ref, hidden_ref, preact_ref, grad_pre_ref = refs[count + 4 :]
    total = tree_sum([ref[...].astype(F32) for ref in refs[:count]])
    row, scale = scale_columns(degrees_ref[...], total.shape[1])
    hidden = scale * total
    weight = weight_ref[...]
    upper, lower = split_two(hidden)
    preact = dot(upper, weight) + dot(lower, weight) + bias_ref[...]
    logistic = 1.0 / (1.0 + jnp.exp(-preact))
    grad_pre = cotangent_ref[...].astype(F32) * logistic * (1.0 + preact * (1.0 - logistic))
    upper, lower = split_two(grad_pre)
    across = ((1,), (1,))
    back = dot(weight, upper, across) + dot(weight, lower, across)
    outgoing_ref[...] = (row * back).astype(BF16)
    hidden_ref[...] = hidden
    preact_ref[...] = preact
    grad_pre_ref[...] = grad_pre


def layer(shares, degrees_row, weight, bias_row, cotangent):
    nodes = degrees_row.shape[1]
    depth, width = weight.shape
    return pl.pallas_call(
        functools.partial(layer_kernel, len(shares)),
        out_shape=[
            jax.ShapeDtypeStruct((depth, nodes), BF16),
            jax.ShapeDtypeStruct((nodes, depth), F32),
            jax.ShapeDtypeStruct((nodes, width), F32),
            jax.ShapeDtypeStruct((nodes, width), F32),
        ],
        compiler_params=params(),
        name="layer",
    )(*shares, degrees_row, weight, bias_row, cotangent)


def activations_kernel(preact_ref, out_ref):
    preact = preact_ref[...]
    out_ref[...] = (preact / (1.0 + jnp.exp(-preact))).astype(BF16)


def activations_of(preact):
    return pl.pallas_call(
        activations_kernel,
        out_shape=jax.ShapeDtypeStruct(preact.shape, BF16),
        compiler_params=params(),
        name="activations",
    )(preact)


def terms_kernel(hidden_ref, grad_pre_ref, *refs):
    outs, terms_ref = refs[:-1], refs[-1]
    grad_pre = grad_pre_ref[...]
    grads = split_two(grad_pre)
    upper, lower = split_two(jnp.transpose(hidden_ref[...]))
    terms_ref[...] = dot(upper, grads[0]) + dot(lower, grads[0]) + dot(upper, grads[1])
    bias_term = jnp.sum(grad_pre, axis=0, keepdims=True)
    pieces = len(outs)
    rows = terms_ref.shape[0] // pieces
    for step, out_ref in enumerate(outs):
        start = pl.multiple_of(other(lax.axis_index("row"), step, pieces) * rows, 8)
        out_ref[0:rows, :] = terms_ref[pl.ds(start, rows), :]
        out_ref[rows:, :] = jnp.broadcast_to(bias_term, (16, bias_term.shape[1]))


def terms_of(hidden, grad_pre):
    pieces = lax.axis_size("row")
    depth, width = hidden.shape[1], grad_pre.shape[1]
    return pl.pallas_call(
        terms_kernel,
        out_shape=[jax.ShapeDtypeStruct((depth // pieces + 16, width), F32)] * pieces,
        scratch_shapes=[pltpu.VMEM((depth, width), F32)],
        compiler_params=params(),
        name="weight_terms",
    )(hidden, grad_pre)


def pack_kernel(outgoing_ref, *refs):
    pieces, out_ref = refs[:-1], refs[-1]
    depth = outgoing_ref.shape[0]
    out_ref[0:depth, :] = outgoing_ref[...]
    out_ref[depth:, :] = tree_sum([piece[...] for piece in pieces]).astype(BF16)


def pack(outgoing, pieces):
    depth, nodes = outgoing.shape
    return pl.pallas_call(
        pack_kernel,
        out_shape=jax.ShapeDtypeStruct((depth + pieces[0].shape[0], nodes), BF16),
        compiler_params=params(),
        name="pack",
    )(outgoing, *pieces)


def tree_sum(values):
    while len(values) > 1:
        values = [left + right for left, right in zip(values[::2], values[1::2])] + (
            values[-1:] if len(values) % 2 else []
        )
    return values[0]


def sum_kernel(depth, *refs):
    refs[-1][...] = tree_sum([ref[depth:, :].astype(F32) for ref in refs[:-1]]).astype(BF16)


def sum_terms(parcels, depth):
    rows, width = parcels[0].shape
    return pl.pallas_call(
        functools.partial(sum_kernel, depth),
        out_shape=jax.ShapeDtypeStruct((rows - depth, width), BF16),
        compiler_params=params(),
        name="sum_terms",
    )(*parcels)


def stack_kernel(*refs):
    for step, ref in enumerate(refs[:-1]):
        refs[-1][step] = ref[...]


def stack_line(items):
    return pl.pallas_call(
        stack_kernel,
        out_shape=jax.ShapeDtypeStruct((len(items),) + items[0].shape, BF16),
        compiler_params=params(),
        name="stack_line",
    )(*items)


def backward_kernel(steps, chosen, pieces, has_totals, dense_ref, *refs):
    count = len(steps)
    parcels, stacks = refs[:count], refs[count : 2 * count]
    inputs, outs = refs[2 * count : -len(chosen)], refs[-len(chosen) :]
    terms = inputs[len(chosen) if has_totals else 0 :]
    high, low, nodes, _ = dense_ref.shape
    row, line, plane = spot(low)
    for index, piece in enumerate(chosen):
        columns = piece_columns(other(row, piece, pieces), nodes)
        total = inputs[index][...] if has_totals else None
        for step, parcel_ref, stack_ref in zip(steps, parcels, stacks):
            origin = source(plane, step, low)
            depth = stack_ref.shape[1]
            for hop in range(high):
                values = stack_ref[hop - 1] if hop else parcel_ref[0:depth, :]
                term = dot(values, dense_ref[source(line, hop, high), origin, :, columns])
                total = term if total is None else total + term
        outs[index][0:depth, :] = total.astype(outs[index].dtype)
        if terms and piece:
            outs[index][depth:, :] = tree_sum([ref[...].astype(F32) for ref in terms]).astype(BF16)


def backward(dense, parcels, stacks, totals, terms=(), chosen=None):
    nodes, slots = dense.shape[2:]
    pieces = slots // nodes
    chosen = tuple(range(pieces)) if chosen is None else chosen
    depth = next(iter(stacks.values())).shape[1]
    inputs = list(parcels.values()) + list(stacks.values()) + list(totals) + list(terms)

    def shape_of(piece):
        if terms and piece:
            return jax.ShapeDtypeStruct((depth + terms[0].shape[0], nodes), BF16)
        return jax.ShapeDtypeStruct((depth, nodes), F32)

    return pl.pallas_call(
        functools.partial(backward_kernel, tuple(stacks), chosen, pieces, bool(totals)),
        out_shape=[shape_of(piece) for piece in chosen],
        in_specs=[pl.BlockSpec(memory_space=pltpu.VMEM)] * (1 + len(inputs)),
        compiler_params=params(),
        name="backward_product",
    )(dense, *inputs)


def finish_kernel(pieces, degrees_ref, own_ref, sent_ref, *refs):
    shares, outs = refs[: pieces - 1], refs[pieces - 1 :]
    total = own_ref[...]
    depth = total.shape[0]
    for share in shares:
        total = total + share[0:depth, :].astype(F32)
    row = lax.rsqrt(degrees_ref[...].astype(F32))
    outs[0][...] = jnp.transpose(row * total).astype(BF16)
    rows = depth // pieces
    for step, ref in enumerate((sent_ref, *shares)):
        start = pl.multiple_of(source(lax.axis_index("row"), step, pieces) * rows, 8)
        outs[1][pl.ds(start, rows), :] = ref[depth : depth + rows, :].astype(F32)
    outs[2][...] = sent_ref[depth + rows : depth + rows + 16, :].astype(F32)[0:1]


def finish(degrees_row, own, sent, shares):
    depth, nodes = own.shape
    width = sent.shape[1]
    return pl.pallas_call(
        functools.partial(finish_kernel, len(shares) + 1),
        out_shape=[
            jax.ShapeDtypeStruct((nodes, depth), BF16),
            jax.ShapeDtypeStruct((depth, width), F32),
            jax.ShapeDtypeStruct((1, width), F32),
        ],
        compiler_params=params(),
        name="finish",
    )(degrees_row, own, sent, *shares)


def far_first(size):
    return range(size - 1, 0, -1)


def per_device(
    features, weight, bias_vector, cotangent, degrees, adjacency_tiles, tile_positions, tile_counts
):
    rows = lax.axis_size("row")
    cols = lax.axis_size("col")
    nodes = features.shape[0]
    per_part = nodes // BLOCK
    row_slots = cols * per_part
    col_slots = rows * per_part
    low = 4 if cols % 4 == 0 else 1
    high = cols // low

    degrees_row = degrees[None, :]

    def over_row(values, step):
        pairs = [(index, other(index, step, rows)) for index in range(rows)]
        return lax.ppermute(values, "row", pairs)

    def over_plane(values, step):
        pairs = [
            (index, index // low * low + other(index % low, step, low)) for index in range(cols)
        ]
        return lax.ppermute(values, "col", pairs)

    def over_line(values, step):
        pairs = [
            (index, other(index // low, step, high) * low + index % low) for index in range(cols)
        ]
        return lax.ppermute(values, "col", pairs)

    steps = range(1, rows)
    degrees_all = [degrees] + [over_row(degrees, step) for step in steps]
    features_all = [features] + [over_row(features, step) for step in steps]
    dense = densify(
        tile_positions, tile_counts, adjacency_tiles[0, 0], row_slots, col_slots
    ).reshape(high, low, nodes, col_slots * BLOCK)

    inputs = [values[None, :] for values in degrees_all] + features_all
    products, scaled = forward(dense, inputs, ((low - 1, True),), scaling=True)
    far_ones = tuple((step, True) for step in far_first(low - 1))
    rest = ((0, True),) + tuple((step, False) for step in (*far_first(low), 0))
    for wanted in (far_ones, rest):
        if wanted:
            products |= forward(dense, scaled, wanted)[0]
    onward = [products[0, True]] + [over_plane(products[step, True], step) for step in far_first(low)]
    here = [products[0, False]] + [over_plane(products[step, False], step) for step in far_first(low)]
    chunks = combine(onward)
    shares = [over_line(chunks[hop - 1], hop) for hop in far_first(high)]
    outgoing, hidden, preact, grad_pre = layer(here + shares, degrees_row, weight, bias_vector[None, :], cotangent)

    line = [over_line(outgoing, step) for step in far_first(high)][::-1]
    pieces = terms_of(hidden, grad_pre)
    activations = activations_of(preact)
    parcel = pack(outgoing, [pieces[0]] + [over_row(pieces[step], step) for step in range(1, rows)])
    parcels = {0: parcel} | {step: over_plane(parcel, step) for step in far_first(low)}
    line, parcels = lax.optimization_barrier((line, parcels))
    stacked = stack_line(line)
    stacks = {0: stacked} | {step: over_plane(stacked, step) for step in far_first(low)}
    terms = sum_terms([parcels[step] for step in range(low)], weight.shape[0])
    parts = {0: terms} | {step: over_line(terms, step) for step in far_first(high)}
    terms = [parts[step] for step in range(high)]
    steps = list(stacks)
    early, late = (
        ({step: parcels[step] for step in group}, {step: stacks[step] for step in group})
        for group in (steps[: low // 2], steps[low // 2 :])
    )
    totals = backward(dense, *early, [])
    sent = backward(dense, *late, totals[1:], terms, tuple(range(1, rows)))
    totals = backward(dense, *late, totals[:1], (), (0,)) + sent
    returned = [over_row(totals[step], step) for step in range(1, rows)]
    grad_features, grad_weight, grad_bias = finish(degrees_row, totals[0], totals[1], returned)
    return activations, grad_features, grad_weight, grad_bias[0]


def solution(mesh):
    placed = (
        P(("row", "col"), None),
        P(),
        P(),
        P(("row", "col"), None),
        P(("row", "col")),
        P("row", "col", None, None, None),
        P("row", "col", None),
        P("row", "col"),
    )
    return jax.shard_map(
        per_device,
        mesh=mesh,
        in_specs=placed,
        out_specs=(P(("row", "col"), None), P(("row", "col"), None), P(), P()),
        check_vma=False,
    )
```
